256 devices in a mesh: dp: 16 (over x_hi, y, core), seq: 16 (over z, x_lo).
Axes of the slice: x: 4 (x_hi: 2, x_lo: 2; x = x_hi * 2 + x_lo), y: 4, z: 8, core: 2. Of those that a mesh axis runs over, the one named last changes fastest.
Arguments:
- hidden_states: bfloat16 [16, 4096, 4096], P('dp', 'seq'), may hold values from -24 to 24
- query_weight: bfloat16 [4096, 2048], P('dp'), may hold values from -0.5 to 0.5
- key_matrix: bfloat16 [4096, 512], P('dp'), may hold values from -0.5 to 0.5
- value_matrix: bfloat16 [4096, 512], P('dp'), may hold values from -0.09375 to 0.09375
- context_lengths: int32 [16], P('dp'), may hold values from 128 to 4096, as said below
Outputs:
- attended: bfloat16 [16, 4096, 2048], P('dp', 'seq')
The draws below stay inside these ranges and needn't reach their ends.
Inputs may be any that keep to these rules, and one draw needn't show every extreme that they name: `context_lengths`: every length is a multiple of 128, and some context has length 4096.
All inputs are finite; a program needn't handle non-finite values.
Results may differ from the reference program's by a relative error of at most 0.0072.
Values may be sent and summed in bfloat16 or wider, within the bound.
A program may use at most 128 MiB of HBM per device.

```python
import jax
import jax.numpy as jnp
from jax import lax

MODEL_WIDTH = 4096
QUERY_HEADS = 16
KEY_VALUE_HEADS = 4
HEAD_WIDTH = 128
WINDOW_TOKENS = 2048
BLOCK = 128
CONTEXT_SLOTS = 4096
CONTEXTS = 16


def draw_hidden_states(key, part):
    key = jax.random.fold_in(key, 11)
    first = jax.random.fold_in(key, 0)
    shape = (CONTEXTS, CONTEXT_SLOTS, MODEL_WIDTH)
    return jnp.clip(jax.random.normal(first, shape, jnp.float32), -4.0, 4.0).astype(jnp.bfloat16)


def draw_query_weight(key, part):
    key = jax.random.fold_in(key, 21)
    newest_rows = jax.random.normal(key, (MODEL_WIDTH, QUERY_HEADS * HEAD_WIDTH), jnp.float32) * MODEL_WIDTH ** (-0.5)
    return jnp.clip(newest_rows, -0.5, 0.5).astype(jnp.bfloat16)


def draw_key_matrix(key, part):
    key = jax.random.fold_in(key, 22)
    newest_rows = jax.random.normal(key, (MODEL_WIDTH, KEY_VALUE_HEADS * HEAD_WIDTH), jnp.float32) * MODEL_WIDTH ** (-0.5)
    return jnp.clip(newest_rows, -0.5, 0.5).astype(jnp.bfloat16)


def draw_context_lengths(key, part):
    key = jax.random.fold_in(key, 31)
    first, second = jax.random.split(key)
    block_list = jax.random.randint(first, (CONTEXTS,), 1, CONTEXT_SLOTS // BLOCK + 1) * BLOCK
    picked_index = jax.random.randint(second, (), 0, CONTEXTS)
    return jnp.where(jnp.arange(CONTEXTS) == picked_index, CONTEXT_SLOTS, block_list).astype(jnp.int32)


def level_of(rng, extent, cuts, smallest, top_value):
    loudness = 1.0
    for dim, shards_of in cuts:
        draws = jax.random.uniform(jax.random.fold_in(jax.random.fold_in(rng, 6), dim), (shards_of,), jnp.float32, smallest / len(cuts), top_value / len(cuts))
        loudness = loudness * jnp.repeat(jnp.exp(draws), extent[dim] // shards_of).reshape((-1,) + (1,) * (len(extent) - 1 - dim))
    return loudness


def normal_values(own_key, dims, scale, most, cuts=(), kind=jnp.bfloat16):
    level = level_of(own_key, dims, cuts, -0.22, 0.18) if cuts else 1.0
    array = jax.random.normal(own_key, dims, jnp.float32) * scale * level
    return jnp.minimum(jnp.maximum(array, -most), most).astype(kind)


def setup_inputs(seed: int = 0) -> dict:
    streams_of = jax.random.split(jax.random.key(seed), 6)
    return {
        "hidden_states": draw_hidden_states(jax.random.fold_in(streams_of[5], 71), 0),
        "query_weight": draw_query_weight(jax.random.fold_in(streams_of[5], 71), 0),
        "key_matrix": draw_key_matrix(jax.random.fold_in(streams_of[5], 71), 0),
        "value_matrix": normal_values(streams_of[3], (MODEL_WIDTH, KEY_VALUE_HEADS * HEAD_WIDTH), MODEL_WIDTH ** -0.5, 0.09375, ((0, 16),)),
        "context_lengths": draw_context_lengths(jax.random.fold_in(streams_of[5], 71), 0),
    }


rope_base = 10000.0
negative_bound = -1e30


def apply_rotary(values_in, positions):
    half = HEAD_WIDTH // 2
    freq = rope_base ** (-(jnp.arange(half, dtype=jnp.float32) * 2.0 / HEAD_WIDTH))
    angle = positions.astype(jnp.float32)[:, None] * freq[None, :]
    cosine = jnp.cos(angle)[:, None, :]
    sine = jnp.sin(angle)[:, None, :]
    first = values_in[..., :half]
    second = values_in[..., half:]
    return jnp.concatenate([first * cosine - second * sine, second * cosine + first * sine], axis=-1)


def reference(hidden_states, query_weight, key_matrix, value_matrix, context_lengths):
    group_size = QUERY_HEADS // KEY_VALUE_HEADS

    def one_context(index):
        token_rows = hidden_states[index]
        length = context_lengths[index]
        token_positions = jnp.arange(CONTEXT_SLOTS, dtype=jnp.int32)
        query_rows = jnp.dot(token_rows, query_weight, preferred_element_type=jnp.float32).reshape(CONTEXT_SLOTS, QUERY_HEADS, HEAD_WIDTH)
        key_row_list = jnp.dot(token_rows, key_matrix, preferred_element_type=jnp.float32).reshape(CONTEXT_SLOTS, KEY_VALUE_HEADS, HEAD_WIDTH)
        value_row_list = jnp.dot(token_rows, value_matrix, preferred_element_type=jnp.float32).reshape(CONTEXT_SLOTS, KEY_VALUE_HEADS, HEAD_WIDTH)
        query_rows = apply_rotary(query_rows, token_positions).astype(jnp.bfloat16).reshape(CONTEXT_SLOTS, KEY_VALUE_HEADS, group_size, HEAD_WIDTH)
        key_row_list = apply_rotary(key_row_list, token_positions).astype(jnp.bfloat16)
        value_row_list = value_row_list.astype(jnp.bfloat16)
        padded_keys = jnp.concatenate([jnp.zeros((WINDOW_TOKENS, KEY_VALUE_HEADS, HEAD_WIDTH), jnp.bfloat16), key_row_list], axis=0)
        padded_values = jnp.concatenate([jnp.zeros((WINDOW_TOKENS, KEY_VALUE_HEADS, HEAD_WIDTH), jnp.bfloat16), value_row_list], axis=0)

        def one_block(begin):
            query_block = lax.dynamic_slice_in_dim(query_rows, begin, BLOCK, 0).astype(jnp.float32)
            key_block = lax.dynamic_slice_in_dim(padded_keys, begin, WINDOW_TOKENS + BLOCK, 0).astype(jnp.float32)
            value_block = lax.dynamic_slice_in_dim(padded_values, begin, WINDOW_TOKENS + BLOCK, 0).astype(jnp.float32)
            query_positions = begin + jnp.arange(BLOCK, dtype=jnp.int32)
            key_pos = begin - WINDOW_TOKENS + jnp.arange(WINDOW_TOKENS + BLOCK, dtype=jnp.int32)
            scores = jnp.einsum("qgrd,kgd->grqk", query_block, key_block) * (HEAD_WIDTH ** -0.5)
            visible = (key_pos[None, :] <= query_positions[:, None]) & (query_positions[:, None] - key_pos[None, :] < WINDOW_TOKENS)
            visible = visible & (key_pos[None, :] >= 0) & (key_pos[None, :] < length)
            visible = visible[None, None]
            masked = jnp.where(visible, scores, negative_bound)
            top = jnp.max(masked, axis=-1, keepdims=True)
            weights = jnp.where(visible, jnp.exp(masked - top), 0.0)
            total = jnp.sum(weights, axis=-1)
            weights_bf = weights.astype(jnp.bfloat16).astype(jnp.float32)
            summed = jnp.einsum("grqk,kgd->grqd", weights_bf, value_block)
            valid = query_positions < length
            safe = jnp.where(valid[None, None, :], total, 1.0)
            result = summed / safe[..., None]
            result = jnp.where(valid[None, None, :, None], result, 0.0)
            return jnp.transpose(result, (2, 0, 1, 3)).reshape(BLOCK, QUERY_HEADS * HEAD_WIDTH).astype(jnp.bfloat16)

        starts = jnp.arange(CONTEXT_SLOTS // BLOCK, dtype=jnp.int32) * BLOCK
        return lax.map(one_block, starts).reshape(CONTEXT_SLOTS, QUERY_HEADS * HEAD_WIDTH)

    return lax.map(one_context, jnp.arange(CONTEXTS, dtype=jnp.int32))
```

```python
import functools

import jax
import jax.numpy as jnp
from jax import lax
from jax.experimental import pallas as pl
from jax.experimental.pallas import tpu as pltpu
from jax.sharding import PartitionSpec as P

HEAD_WIDTH = 128
WINDOW_TOKENS = 2048
SLAB = 256
SHARD = 512
SHARDS = 8
DEPTH = SHARD * SHARDS
GROUP = 4
SLOTS = WINDOW_TOKENS // SLAB + 1
LEVELS = 4
SCORE_SCALE = HEAD_WIDTH**-0.5 * 1.4426950408889634
rope_base = 10000.0
negative_bound = -1e30
MESH = pl.DeviceIdType.MESH

PIECES = ("k", "v", "q0", "q1")
SWAP, YP, YM, XB, YP_A, YM_A, YP_B, YM_B, XB_A = range(9)
PER_PIECE = 9
HALO = PER_PIECE * len(PIECES)
OUT = HALO + 4 * LEVELS
X_SWAP = OUT + 2
FLOWS = X_SWAP + 1


def rope_tables(seq):
    half = HEAD_WIDTH // 2
    positions = seq * SLAB + jnp.arange(SLAB, dtype=jnp.int32)
    freq = rope_base ** (-(jnp.arange(half, dtype=jnp.float32) * 2.0 / HEAD_WIDTH))
    angle = positions.astype(jnp.float32)[:, None] * freq[None, :]
    cosine, sine = jnp.cos(angle), jnp.sin(angle)
    return jnp.concatenate([cosine, cosine], 1), jnp.concatenate([-sine, sine], 1)


def kernel(
    x_ref, wq_ref, wk_ref, wv_ref, cos_ref, sin_ref, out_ref,
    xbuf, wk, wv, wq0, wq1, kbuf, vbuf, qbuf, stage, acc, top, total,
    send, recv, local,
):
    dp, seq = lax.axis_index("dp"), lax.axis_index("seq")
    hi, y, core = dp // 8, (dp // 2) % 4, dp % 2
    z, lo = seq // 2, seq % 2
    up, down, across = (y + 1) % 4, (y + 3) % 4, (y + 2) % 4

    def device(hi, y, core, z, lo):
        return (hi * 8 + y * 2 + core, z * 2 + lo)

    partner = device(hi, y, 1 - core, z, lo)
    y_next, y_prev = device(hi, up, core, z, lo), device(hi, down, core, z, lo)
    x_far = device(1 - hi, y, core, z, 1 - lo)
    x_near = device(hi, y, core, z, 1 - lo)
    z_next, z_prev = device(hi, y, core, (z + 1) % 8, lo), device(hi, y, core, (z + 7) % 8, lo)

    def remote(src, dst, flow, to):
        return pltpu.make_async_remote_copy(
            src_ref=src, dst_ref=dst, send_sem=send.at[flow], recv_sem=recv.at[flow],
            device_id=to, device_id_type=MESH,
        )

    def shard(g, yy):
        return g * 4 + yy

    def rows(w, s, first=0, count=SHARD):
        return w.at[pl.ds(pl.multiple_of(s * SHARD + first, 256), count)]

    def columns(ref, c, j, width):
        if ref is wq_ref:
            return ref.at[:, pl.ds(pl.multiple_of(c * 1024 + j * 512, 512), width)]
        return ref.at[:, pl.ds(pl.multiple_of(c * 256, 256), width)]

    weights = {
        "k": (wk_ref, wk, 0, 256), "v": (wv_ref, wv, 0, 256),
        "q0": (wq_ref, wq0, 0, 512), "q1": (wq_ref, wq1, 1, 512),
    }

    mine = shard(hi, y)

    class Piece:
        def __init__(self, name):
            self.index = PIECES.index(name)
            self.ref, self.w, self.j, self.width = weights[name]
            base = PER_PIECE * self.index
            w = self.w
            self.local = pltpu.make_async_copy(
                columns(self.ref, core, self.j, self.width),
                w.at[pl.ds(pl.multiple_of(mine * SHARD + core * 256, 256), 256)],
                local.at[self.index],
            )
            theirs = w.at[pl.ds(pl.multiple_of(mine * SHARD + core * 256, 256), 256)]
            ours = w.at[pl.ds(pl.multiple_of(mine * SHARD + (1 - core) * 256, 256), 256)]
            self.swap_out = remote(
                columns(self.ref, 1 - core, self.j, self.width), theirs, base + SWAP, partner
            )
            self.swap_in = remote(ours, ours, base + SWAP, partner)

            def both(flow, to, out_part, in_part):
                return (
                    remote(out_part, out_part, base + flow, to),
                    remote(in_part, in_part, base + flow, to),
                )

            own = rows(w, mine)
            far = shard(1 - hi, y)
            self.flows = {
                YP: both(YP, y_next, own, rows(w, shard(hi, down))),
                YM: both(YM, y_prev, own, rows(w, shard(hi, up))),
                XB: both(XB, x_far, own, rows(w, far)),
                YP_A: both(YP_A, y_next, rows(w, shard(hi, down), 0, 256), rows(w, shard(hi, across), 0, 256)),
                YM_A: both(YM_A, y_prev, rows(w, shard(hi, up), 256, 256), rows(w, shard(hi, across), 256, 256)),
                YP_B: both(YP_B, y_next, rows(w, far), rows(w, shard(1 - hi, down))),
                YM_B: both(YM_B, y_prev, rows(w, far), rows(w, shard(1 - hi, up))),
                XB_A: both(XB_A, x_far, rows(w, shard(hi, across)), rows(w, shard(1 - hi, across))),
            }

        def go(self, *flows):
            for f in flows:
                self.flows[f][0].start()

        def got(self, *flows):
            for f in flows:
                self.flows[f][1].wait_recv()

        def p0(self):
            self.local.wait()
            self.swap_in.wait_recv()
            self.go(XB, YP, YM)

        def p1(self):
            self.got(XB)
            self.go(YP_B, YM_B)
            self.got(YP)
            self.go(YP_A)
            self.got(YM)
            self.go(YM_A)

        def p2(self):
            self.got(YP_A, YM_A)
            self.go(XB_A)

        def p3(self):
            self.got(YP_B, YM_B, XB_A)

        def finish(self):
            self.swap_out.wait_send()
            for out, _ in self.flows.values():
                out.wait_send()

    k, v, q0, q1 = [Piece(name) for name in PIECES]

    x_local = pltpu.make_async_copy(x_ref, xbuf.at[core], local.at[4])
    k.local.start()
    x_local.start()
    for piece in (v, q0, q1):
        piece.local.start()

    barrier = pltpu.get_barrier_semaphore()
    partners = (partner, y_next, y_prev, x_far, x_near, z_next, z_prev)
    for other in partners:
        pl.semaphore_signal(barrier, inc=1, device_id=other, device_id_type=MESH)
    pl.semaphore_wait(barrier, len(partners))

    x_out = remote(x_ref, xbuf.at[core], X_SWAP, partner)
    x_in = remote(xbuf.at[1 - core], xbuf.at[1 - core], X_SWAP, partner)
    k.swap_out.start()
    x_out.start()
    for piece in (v, q0, q1):
        piece.swap_out.start()

    def rotate(values):
        return values * cos_ref[...] + pltpu.roll(values, HEAD_WIDTH // 2, 1) * sin_ref[...]

    class Halo:
        def __init__(self, which, buf):
            self.base = HALO + which * 2 * LEVELS
            self.buf = buf

        def z_send(self, level):
            return remote(self.buf.at[2 * level], self.buf.at[2 * level + 2], self.base + level, z_next)

        def near_send(self, level, step):
            return remote(self.buf.at[2 * level], self.buf.at[2 * step + 1], self.base + LEVELS + step, x_near)

        def level(self, level):
            if level > 0:
                self.z_send(level - 1).wait_recv()
            if level < LEVELS:
                self.z_send(level).start()

                @pl.when(lo == 0)
                def _():
                    self.near_send(level, level).start()

            if level > 0:

                @pl.when(lo == 1)
                def _():
                    self.near_send(level, level - 1).start()

        def near(self, step):
            self.near_send(step, step).wait_recv()

        def finish(self):
            for i in range(LEVELS):
                self.z_send(i).wait_send()
                self.near_send(i, i).wait_send()

    halo_k, halo_v = Halo(0, kbuf), Halo(1, vbuf)

    def project_k():
        @pl.loop(0, 2)
        def _(ctx):
            full = jnp.dot(xbuf[ctx], wk[...], preferred_element_type=jnp.float32)
            for j in range(2):
                head = full[:, j * HEAD_WIDTH : (j + 1) * HEAD_WIDTH]
                kbuf[0, ctx, :, j * HEAD_WIDTH : (j + 1) * HEAD_WIDTH] = rotate(head).astype(jnp.bfloat16)

    def project_v():
        @pl.loop(0, 2)
        def _(ctx):
            full = jnp.dot(xbuf[ctx], wv[...], preferred_element_type=jnp.float32)
            vbuf[0, ctx] = full.astype(jnp.bfloat16)

    def project_q(j, w):
        @pl.loop(0, 2)
        def _(ctx):
            full = jnp.dot(xbuf[ctx], w[...], preferred_element_type=jnp.float32)
            for h in range(GROUP):
                head = full[:, h * HEAD_WIDTH : (h + 1) * HEAD_WIDTH]
                qbuf[j, ctx, h * SLAB : (h + 1) * SLAB] = rotate(head).astype(jnp.bfloat16)

    tall = GROUP * SLAB

    def attend(j, ctx):
        lanes = slice(j * HEAD_WIDTH, (j + 1) * HEAD_WIDTH)
        contract = (((1,), (1,)), ((), ()))

        def scores(d):
            return lax.dot_general(
                qbuf[j, ctx], kbuf[d, ctx, :, lanes], contract, preferred_element_type=jnp.float32
            )

        def fold(p):
            return p[:, :128] + p[:, 128:]

        row = lax.broadcasted_iota(jnp.int32, (tall, SLAB), 0) % SLAB
        col = lax.broadcasted_iota(jnp.int32, (tall, SLAB), 1)

        s = jnp.where(col <= row, scores(0), negative_bound)
        m = jnp.max(s, axis=1, keepdims=True)
        p = jnp.exp2((s - m) * SCORE_SCALE)
        top[...] = jnp.broadcast_to(m, (tall, 128))
        total[...] = fold(p)
        acc[...] = jnp.dot(p.astype(jnp.bfloat16), vbuf[0, ctx, :, lanes], preferred_element_type=jnp.float32)

        def update(d, masked):
            s = scores(d)
            if masked:
                s = jnp.where(col > row, s, negative_bound)
            old = top[...]
            m = jnp.maximum(old, jnp.max(s, axis=1, keepdims=True))
            factor = jnp.exp2((old - m) * SCORE_SCALE)
            p = jnp.exp2((s - jnp.concatenate([m, m], 1)) * SCORE_SCALE)
            top[...] = m
            total[...] = total[...] * factor + fold(p)
            acc[...] = acc[...] * factor + jnp.dot(
                p.astype(jnp.bfloat16), vbuf[d, ctx, :, lanes], preferred_element_type=jnp.float32
            )

        lax.fori_loop(1, jnp.minimum(seq, SLOTS - 2) + 1, lambda d, c: (update(d, False), c)[1], 0)

        @pl.when(seq >= SLOTS - 1)
        def _():
            update(SLOTS - 1, True)

        result = acc[...] / jnp.sum(total[...], axis=1, keepdims=True)
        for h in range(GROUP):
            stage[j, ctx, :, h * HEAD_WIDTH : (h + 1) * HEAD_WIDTH] = result[
                h * SLAB : (h + 1) * SLAB
            ].astype(jnp.bfloat16)

    def out_columns(j):
        return out_ref.at[:, pl.ds(pl.multiple_of(core * 1024 + j * 512, 512), 512)]

    def out_arrive(j):
        theirs = out_ref.at[:, pl.ds(pl.multiple_of((1 - core) * 1024 + j * 512, 512), 512)]
        return remote(stage.at[j, core], theirs, OUT + j, partner)

    def out_local(j):
        return pltpu.make_async_copy(stage.at[j, core], out_columns(j), local.at[5 + j])

    def out_remote(j):
        return remote(stage.at[j, 1 - core], out_columns(j), OUT + j, partner)

    k.p0()
    k.p1()
    k.p2()
    v.p0()
    x_local.wait()
    x_in.wait_recv()
    k.p3()
    project_k()
    halo_k.level(0)
    v.p1()
    halo_k.level(1)
    v.p2()
    q0.p0()
    v.p3()
    project_v()
    halo_v.level(0)
    halo_k.level(2)
    halo_k.level(3)
    q0.p1()
    halo_v.level(1)
    halo_k.level(4)
    halo_v.level(2)
    q0.p2()
    q1.p0()
    halo_v.level(3)
    q0.p3()
    project_q(0, wq0)
    halo_v.level(4)
    for step in range(LEVELS):
        halo_k.near(step)
        halo_v.near(step)
    attend(0, 1 - core)
    q1.p1()
    attend(0, core)
    out_remote(0).start()
    out_local(0).start()
    q1.p2()
    q1.p3()
    project_q(1, wq1)
    attend(1, 1 - core)
    out_remote(1).start()
    attend(1, core)
    out_local(1).start()

    for piece in (k, v, q0, q1):
        piece.finish()
    x_out.wait_send()
    halo_k.finish()
    halo_v.finish()
    for j in range(2):
        out_local(j).wait()
        out_remote(j).wait_send()
        out_arrive(j).wait_recv()


def body(hidden_states, query_weight, key_matrix, value_matrix, context_lengths):
    x = hidden_states[0]
    seq = lax.axis_index("seq")
    cosine, sine = rope_tables(seq)
    any_space = pl.BlockSpec(memory_space=pl.ANY)
    vmem = pl.BlockSpec(memory_space=pltpu.VMEM)
    bf16, f32 = jnp.bfloat16, jnp.float32
    tall = GROUP * SLAB
    attended = pl.pallas_call(
        kernel,
        out_shape=jax.ShapeDtypeStruct((SLAB, 2048), bf16),
        in_specs=[any_space] * 4 + [vmem] * 2,
        out_specs=any_space,
        scratch_shapes=[
            pltpu.VMEM((2, SLAB, DEPTH), bf16),
            pltpu.VMEM((DEPTH, 256), bf16),
            pltpu.VMEM((DEPTH, 256), bf16),
            pltpu.VMEM((DEPTH, 512), bf16),
            pltpu.VMEM((DEPTH, 512), bf16),
            pltpu.VMEM((SLOTS, 2, SLAB, 256), bf16),
            pltpu.VMEM((SLOTS, 2, SLAB, 256), bf16),
            pltpu.VMEM((2, 2, tall, HEAD_WIDTH), bf16),
            pltpu.VMEM((2, 2, SLAB, 512), bf16),
            pltpu.VMEM((tall, HEAD_WIDTH), f32),
            pltpu.VMEM((tall, HEAD_WIDTH), f32),
            pltpu.VMEM((tall, HEAD_WIDTH), f32),
            pltpu.SemaphoreType.DMA((FLOWS,)),
            pltpu.SemaphoreType.DMA((FLOWS,)),
            pltpu.SemaphoreType.DMA((7,)),
        ],
        compiler_params=pltpu.CompilerParams(
            collective_id=0, has_side_effects=True, vmem_limit_bytes=56 * 2**20
        ),
        name="gather_project_attend",
    )(x, query_weight, key_matrix, value_matrix, cosine, sine)
    positions = seq * SLAB + jnp.arange(SLAB, dtype=jnp.int32)
    valid = positions < context_lengths[0]
    return jnp.where(valid[:, None], attended, jnp.zeros_like(attended))[None]


def solution(mesh):
    return jax.shard_map(
        body,
        mesh=mesh,
        in_specs=(P("dp", "seq", None), P("dp", None), P("dp", None), P("dp", None), P("dp")),
        out_specs=P("dp", "seq", None),
        check_vma=False,
    )
```

```python
import functools

import jax
import jax.numpy as jnp
from jax import lax
from jax.experimental import pallas as pl
from jax.experimental.pallas import tpu as pltpu
from jax.sharding import PartitionSpec as P

HEAD_WIDTH = 128
SLAB = 256
PAIR = 2 * SLAB
SHARD = 512
SHARDS = 8
DEPTH = SHARD * SHARDS
LEVELS = 4
TALL = 4 * SLAB
X_CHUNKS = 4
SCORE_SCALE = HEAD_WIDTH**-0.5 * 1.4426950408889634
rope_base = 10000.0
negative_bound = -1e30
MESH = pl.DeviceIdType.MESH

PIECES = ("k", "v", "qa", "qb")
SWAP, YP, YM, XB, YP_A, YM_A, YP_B, YM_B, XB_A = range(9)
PER_PIECE = 9
HALO = PER_PIECE * len(PIECES)
PER_HALO = LEVELS + 1
OUT = HALO + 2 * PER_HALO
PER_OUT = 3
X_SWAP = OUT + 2 * PER_OUT
X_NEAR = X_SWAP + 1
X_FORWARD = X_NEAR + X_CHUNKS
FLOWS = X_FORWARD + 1


def rope_tables(z):
    half = HEAD_WIDTH // 2
    positions = z * PAIR + jnp.arange(PAIR, dtype=jnp.int32)
    freq = rope_base ** (-(jnp.arange(half, dtype=jnp.float32) * 2.0 / HEAD_WIDTH))
    angle = positions.astype(jnp.float32)[:, None] * freq[None, :]
    cosine, sine = jnp.cos(angle), jnp.sin(angle)
    return (
        jnp.concatenate([cosine, cosine], 1).reshape(2, SLAB, HEAD_WIDTH),
        jnp.concatenate([-sine, sine], 1).reshape(2, SLAB, HEAD_WIDTH),
    )


def kernel(
    x_ref, wq_ref, wk_ref, wv_ref, cos_ref, sin_ref, out_ref,
    xbuf, wk, wv, wqa, wqb, khead, vhead, kbuf, vbuf, qbuf, stage, acc, top, total,
    send, recv, local,
):
    dp, seq = lax.axis_index("dp"), lax.axis_index("seq")
    hi, y, core = dp // 8, (dp // 2) % 4, dp % 2
    z, lo = seq // 2, seq % 2
    pick = (lo + hi) % 2
    up, down, across = (y + 1) % 4, (y + 3) % 4, (y + 2) % 4

    def device(hi, y, core, z, lo):
        return (hi * 8 + y * 2 + core, z * 2 + lo)

    partner = device(hi, y, 1 - core, z, lo)
    y_next, y_prev = device(hi, up, core, z, lo), device(hi, down, core, z, lo)
    x_far = device(1 - hi, y, core, z, 1 - lo)
    x_near = device(hi, y, core, z, 1 - lo)
    x_diag = device(hi, y, 1 - core, z, 1 - lo)
    z_next, z_prev = device(hi, y, core, (z + 1) % 8, lo), device(hi, y, core, (z + 7) % 8, lo)

    def remote(src, dst, flow, to):
        return pltpu.make_async_remote_copy(
            src_ref=src, dst_ref=dst, send_sem=send.at[flow], recv_sem=recv.at[flow],
            device_id=to, device_id_type=MESH,
        )

    def shard(g, yy):
        return g * 4 + yy

    def rows(w, s, first=0, count=SHARD):
        return w.at[pl.ds(pl.multiple_of(s * SHARD + first, 256), count)]

    def columns(name, c):
        if name == "k":
            return wk_ref.at[:, pl.ds(pl.multiple_of(c * 256, 256), 256)]
        if name == "v":
            return wv_ref.at[:, pl.ds(pl.multiple_of(c * 256, 256), 256)]
        first = (2 * c + pick) * 512 + (256 if name == "qb" else 0)
        return wq_ref.at[:, pl.ds(pl.multiple_of(first, 256), 256)]

    buffers = {"k": wk, "v": wv, "qa": wqa, "qb": wqb}
    mine = shard(hi, y)

    class Piece:
        def __init__(self, name):
            self.index = PIECES.index(name)
            w = self.w = buffers[name]
            base = PER_PIECE * self.index
            theirs = w.at[pl.ds(pl.multiple_of(mine * SHARD + core * 256, 256), 256)]
            ours = w.at[pl.ds(pl.multiple_of(mine * SHARD + (1 - core) * 256, 256), 256)]
            self.local = pltpu.make_async_copy(columns(name, core), theirs, local.at[self.index])
            self.swap_out = remote(columns(name, 1 - core), theirs, base + SWAP, partner)
            self.swap_in = remote(ours, ours, base + SWAP, partner)

            def both(flow, to, out_part, in_part):
                return (
                    remote(out_part, out_part, base + flow, to),
                    remote(in_part, in_part, base + flow, to),
                )

            own = rows(w, mine)
            far = shard(1 - hi, y)
            self.flows = {
                YP: both(YP, y_next, own, rows(w, shard(hi, down))),
                YM: both(YM, y_prev, own, rows(w, shard(hi, up))),
                XB: both(XB, x_far, own, rows(w, far)),
                YP_A: both(YP_A, y_next, rows(w, shard(hi, down), 0, 256), rows(w, shard(hi, across), 0, 256)),
                YM_A: both(YM_A, y_prev, rows(w, shard(hi, up), 256, 256), rows(w, shard(hi, across), 256, 256)),
                YP_B: both(YP_B, y_next, rows(w, far), rows(w, shard(1 - hi, down))),
                YM_B: both(YM_B, y_prev, rows(w, far), rows(w, shard(1 - hi, up))),
                XB_A: both(XB_A, x_far, rows(w, shard(hi, across)), rows(w, shard(1 - hi, across))),
            }

        def go(self, *flows):
            for f in flows:
                self.flows[f][0].start()

        def got(self, *flows):
            for f in flows:
                self.flows[f][1].wait_recv()

        def p0(self):
            self.local.wait()
            self.swap_in.wait_recv()
            self.go(XB, YP, YM)

        def p1(self):
            self.got(YP)
            self.go(YP_A)
            self.got(YM)
            self.go(YM_A)
            self.got(XB)
            self.go(YP_B, YM_B)

        def p2(self):
            self.got(YP_A, YM_A)
            self.go(XB_A)

        def p3(self):
            self.got(YP_B, YM_B, XB_A)

        def finish(self):
            self.swap_out.wait_send()
            for out, _ in self.flows.values():
                out.wait_send()

    k, v, qa, qb = [Piece(name) for name in PIECES]
    pieces = (k, v, qa, qb)

    x_local = pltpu.make_async_copy(x_ref, xbuf.at[lo, core], local.at[4])
    for piece in pieces:
        piece.local.start()
    x_local.start()

    barrier = pltpu.get_barrier_semaphore()
    partners = (partner, y_next, y_prev, x_far, x_near, x_diag, z_next, z_prev)
    for other in partners:
        pl.semaphore_signal(barrier, inc=1, device_id=other, device_id_type=MESH)
    pl.semaphore_wait(barrier, len(partners))

    x_out = remote(x_ref, xbuf.at[lo, core], X_SWAP, partner)
    x_in = remote(xbuf.at[lo, 1 - core], xbuf.at[lo, 1 - core], X_SWAP, partner)

    def x_near_out(i):
        part = pl.ds(i * (SLAB // X_CHUNKS), SLAB // X_CHUNKS)
        return remote(x_ref.at[part], xbuf.at[lo, core, part], X_NEAR + i, x_near)

    def x_near_in(i):
        part = pl.ds(i * (SLAB // X_CHUNKS), SLAB // X_CHUNKS)
        there = xbuf.at[1 - lo, core, part]
        return remote(there, there, X_NEAR + i, x_near)

    x_forward_out = remote(xbuf.at[1 - lo, core], xbuf.at[1 - lo, core], X_FORWARD, partner)
    x_forward_in = remote(xbuf.at[1 - lo, 1 - core], xbuf.at[1 - lo, 1 - core], X_FORWARD, partner)

    for piece in pieces:
        piece.swap_out.start()
    x_out.start()

    def rotate(values, which):
        return values * cos_ref[which] + pltpu.roll(values, HEAD_WIDTH // 2, 1) * sin_ref[which]

    class Halo:
        def __init__(self, which, heads, buf):
            self.base = HALO + which * PER_HALO
            self.heads, self.buf = heads, buf
            self.near_out = remote(heads.at[1 - pick], buf.at[0, :, lo], self.base + LEVELS, x_near)
            there = buf.at[0, :, 1 - lo]
            self.near_in = remote(there, there, self.base + LEVELS, x_near)

        def near(self):
            self.near_out.start()
            self.buf[0, :, lo] = self.heads[pick]

        def z_send(self, level):
            return remote(self.buf.at[level], self.buf.at[level + 1], self.base + level, z_next)

        def level(self, level):
            if level == 0:
                self.near_in.wait_recv()
            else:
                self.z_send(level - 1).wait_recv()
            if level < LEVELS:
                self.z_send(level).start()

        def finish(self):
            self.near_out.wait_send()
            for i in range(LEVELS):
                self.z_send(i).wait_send()

    halo_k, halo_v = Halo(0, khead, kbuf), Halo(1, vhead, vbuf)

    def project_k():
        @pl.loop(0, 2)
        def _(ctx):
            full = jnp.dot(xbuf[lo, ctx], wk[...], preferred_element_type=jnp.float32)
            for j in range(2):
                head = full[:, j * HEAD_WIDTH : (j + 1) * HEAD_WIDTH]
                khead[j, ctx] = rotate(head, lo).astype(jnp.bfloat16)

    def project_v():
        @pl.loop(0, 2)
        def _(ctx):
            full = jnp.dot(xbuf[lo, ctx], wv[...], preferred_element_type=jnp.float32)
            for j in range(2):
                vhead[j, ctx] = full[:, j * HEAD_WIDTH : (j + 1) * HEAD_WIDTH].astype(jnp.bfloat16)

    def project_q(half, w, side):
        @pl.loop(0, 2)
        def _(ctx):
            full = jnp.dot(xbuf[side, ctx], w[...], preferred_element_type=jnp.float32)
            for h in range(2):
                head = full[:, h * HEAD_WIDTH : (h + 1) * HEAD_WIDTH]
                first = pl.multiple_of(side * PAIR + h * SLAB, SLAB)
                qbuf[half, ctx, pl.ds(first, SLAB)] = rotate(head, side).astype(jnp.bfloat16)

    def scores(queries, keys):
        return lax.dot_general(
            queries, keys, (((1,), (1,)), ((), ())), preferred_element_type=jnp.float32
        )

    def fold(p):
        return sum(p[:, i : i + 128] for i in range(0, p.shape[1], 128))

    def visible(side, first_key, shape, newest):
        token = lax.broadcasted_iota(jnp.int32, shape, 0) % SLAB + side * SLAB
        key = lax.broadcasted_iota(jnp.int32, shape, 1) + first_key
        return key <= token if newest else key > token

    def begin(half, ctx):
        for side in range(2):
            part = slice(side * PAIR, (side + 1) * PAIR)
            count = (side + 1) * SLAB
            keys = kbuf[0, ctx].reshape(PAIR, HEAD_WIDTH)[:count]
            values = vbuf[0, ctx].reshape(PAIR, HEAD_WIDTH)[:count]
            s = scores(qbuf[half, ctx, part], keys)
            s = jnp.where(visible(side, 0, s.shape, True), s, negative_bound)
            m = jnp.max(s, axis=1, keepdims=True)
            p = jnp.exp2((s - m) * SCORE_SCALE)
            top[half, ctx, part] = jnp.broadcast_to(m, (PAIR, 128))
            total[half, ctx, part] = fold(p)
            acc[half, ctx, part] = jnp.dot(
                p.astype(jnp.bfloat16), values, preferred_element_type=jnp.float32
            )

    def update(half, ctx, part, s, values):
        old = top[half, ctx, part]
        m = jnp.maximum(old, jnp.max(s, axis=1, keepdims=True))
        factor = jnp.exp2((old - m) * SCORE_SCALE)
        p = jnp.exp2((s - jnp.concatenate([m] * (s.shape[1] // 128), 1)) * SCORE_SCALE)
        top[half, ctx, part] = m
        total[half, ctx, part] = total[half, ctx, part] * factor + fold(p)
        acc[half, ctx, part] = acc[half, ctx, part] * factor + jnp.dot(
            p.astype(jnp.bfloat16), values, preferred_element_type=jnp.float32
        )

    def middle(half, ctx, level):
        keys = kbuf[level, ctx].reshape(PAIR, HEAD_WIDTH)
        values = vbuf[level, ctx].reshape(PAIR, HEAD_WIDTH)
        update(half, ctx, slice(0, TALL), scores(qbuf[half, ctx], keys), values)

    def oldest(half, ctx):
        for side in range(2):
            part = slice(side * PAIR, (side + 1) * PAIR)
            first = side * SLAB
            keys = kbuf[LEVELS, ctx].reshape(PAIR, HEAD_WIDTH)[first:]
            values = vbuf[LEVELS, ctx].reshape(PAIR, HEAD_WIDTH)[first:]
            s = scores(qbuf[half, ctx, part], keys)
            s = jnp.where(visible(side, first, s.shape, False), s, negative_bound)
            update(half, ctx, part, s, values)

    def attend(half, first, last):
        @pl.loop(0, 2)
        def _(ctx):
            if first == 0:
                begin(half, ctx)
            lax.fori_loop(
                max(first, 1), jnp.minimum(z, min(last, LEVELS - 1)) + 1,
                lambda level, c: (middle(half, ctx, level), c)[1], 0,
            )
            if last == LEVELS:

                @pl.when(z >= LEVELS)
                def _():
                    oldest(half, ctx)

                result = acc[half, ctx] / jnp.sum(total[half, ctx], axis=1, keepdims=True)
                for side in range(2):
                    for h in range(2):
                        first_row = side * PAIR + h * SLAB
                        stage[half, side, ctx, :, h * HEAD_WIDTH : (h + 1) * HEAD_WIDTH] = result[
                            first_row : first_row + SLAB
                        ].astype(jnp.bfloat16)

    def out_columns(half, head):
        return out_ref.at[:, pl.ds(pl.multiple_of(head * 512 + half * 256, 256), 256)]

    head = 2 * core + pick

    def out_flows(half):
        base = OUT + half * PER_OUT
        dst = out_columns(half, head)
        return (
            (remote(stage.at[half, 1 - lo, core], dst, base, x_near), 2 * core + 1 - pick),
            (remote(stage.at[half, 1 - lo, 1 - core], dst, base + 1, x_diag), 2 * (1 - core) + 1 - pick),
            (remote(stage.at[half, lo, 1 - core], dst, base + 2, partner), 2 * (1 - core) + pick),
        )

    def out_local(half):
        return pltpu.make_async_copy(stage.at[half, lo, core], out_columns(half, head), local.at[5 + half])

    def out_start(half):
        for flow, _ in out_flows(half):
            flow.start()
        out_local(half).start()

    def out_finish(half):
        out_local(half).wait()
        for i, (flow, other) in enumerate(out_flows(half)):
            flow.wait_send()
            landed = out_columns(half, other)
            remote(landed, landed, OUT + half * PER_OUT + i, partner).wait_recv()

    k.p0()
    x_near_out(0).start()
    x_near_out(1).start()
    k.p1()
    v.p0()
    k.p2()
    x_local.wait()
    x_in.wait_recv()
    k.p3()
    project_k()
    halo_k.near()
    v.p1()
    qa.p0()
    halo_k.level(0)
    x_near_out(2).start()
    v.p2()
    halo_k.level(1)
    v.p3()
    project_v()
    halo_v.near()
    halo_k.level(2)
    qa.p1()
    qb.p0()
    halo_v.level(0)
    x_near_out(3).start()
    qa.p2()
    halo_k.level(3)
    qa.p3()
    project_q(0, wqa, lo)
    halo_v.level(1)
    qb.p1()
    for i in range(X_CHUNKS):
        x_near_in(i).wait_recv()
    x_forward_out.start()
    halo_k.level(4)
    qb.p2()
    x_forward_in.wait_recv()
    project_q(0, wqa, 1 - lo)
    halo_v.level(2)
    attend(0, 0, 1)
    qb.p3()
    halo_v.level(3)
    project_q(1, wqb, lo)
    project_q(1, wqb, 1 - lo)
    attend(1, 0, 2)
    halo_v.level(4)
    attend(0, 2, 4)
    out_start(0)
    attend(1, 3, 4)
    out_start(1)

    for piece in pieces:
        piece.finish()
    x_out.wait_send()
    for i in range(X_CHUNKS):
        x_near_out(i).wait_send()
    x_forward_out.wait_send()
    halo_k.finish()
    halo_v.finish()
    for half in range(2):
        out_finish(half)


def body(hidden_states, query_weight, key_matrix, value_matrix, context_lengths):
    x = hidden_states[0]
    seq = lax.axis_index("seq")
    cosine, sine = rope_tables(seq // 2)
    any_space = pl.BlockSpec(memory_space=pl.ANY)
    vmem = pl.BlockSpec(memory_space=pltpu.VMEM)
    bf16, f32 = jnp.bfloat16, jnp.float32
    attended = pl.pallas_call(
        kernel,
        out_shape=jax.ShapeDtypeStruct((SLAB, 2048), bf16),
        in_specs=[any_space] * 4 + [vmem] * 2,
        out_specs=any_space,
        scratch_shapes=[
            pltpu.VMEM((2, 2, SLAB, DEPTH), bf16),
            pltpu.VMEM((DEPTH, 256), bf16),
            pltpu.VMEM((DEPTH, 256), bf16),
            pltpu.VMEM((DEPTH, 256), bf16),
            pltpu.VMEM((DEPTH, 256), bf16),
            pltpu.VMEM((2, 2, SLAB, HEAD_WIDTH), bf16),
            pltpu.VMEM((2, 2, SLAB, HEAD_WIDTH), bf16),
            pltpu.VMEM((LEVELS + 1, 2, 2, SLAB, HEAD_WIDTH), bf16),
            pltpu.VMEM((LEVELS + 1, 2, 2, SLAB, HEAD_WIDTH), bf16),
            pltpu.VMEM((2, 2, TALL, HEAD_WIDTH), bf16),
            pltpu.VMEM((2, 2, 2, SLAB, 256), bf16),
            pltpu.VMEM((2, 2, TALL, HEAD_WIDTH), f32),
            pltpu.VMEM((2, 2, TALL, HEAD_WIDTH), f32),
            pltpu.VMEM((2, 2, TALL, HEAD_WIDTH), f32),
            pltpu.SemaphoreType.DMA((FLOWS,)),
            pltpu.SemaphoreType.DMA((FLOWS,)),
            pltpu.SemaphoreType.DMA((7,)),
        ],
        compiler_params=pltpu.CompilerParams(
            collective_id=0, has_side_effects=True, vmem_limit_bytes=56 * 2**20
        ),
        name="gather_project_attend",
    )(x, query_weight, key_matrix, value_matrix, cosine, sine)
    positions = seq * SLAB + jnp.arange(SLAB, dtype=jnp.int32)
    valid = positions < context_lengths[0]
    return jnp.where(valid[:, None], attended, jnp.zeros_like(attended))[None]


def solution(mesh):
    return jax.shard_map(
        body,
        mesh=mesh,
        in_specs=(P("dp", "seq", None), P("dp", None), P("dp", None), P("dp", None), P("dp")),
        out_specs=P("dp", "seq", None),
        check_vma=False,
    )
```

```python
import functools

import jax
import jax.numpy as jnp
from jax import lax
from jax.experimental import pallas as pl
from jax.experimental.pallas import tpu as pltpu
from jax.sharding import PartitionSpec as P

HEAD_WIDTH = 128
SLAB = 256
PAIR = 2 * SLAB
SHARD = 512
SHARDS = 8
DEPTH = SHARD * SHARDS
LEVELS = 4
GROUP = 4
TALL = GROUP * SLAB
X_CHUNKS = 8
SCORE_SCALE = HEAD_WIDTH**-0.5 * 1.4426950408889634
LOG_ROPE_BASE = 9.210340371976184
negative_bound = -1e30
MESH = pl.DeviceIdType.MESH

PIECES = ("k", "v", "qa", "qb")
FLOW_NAMES = (
    "up0", "up1", "down1", "down0", "far0", "far1", "up_near", "down_near",
    "up_far0", "down_far0", "up_far1", "down_far1", "far_across0", "far_across1",
)
SHARD_NAMES = ("below", "above", "opposite", "far", "far_below", "far_above", "far_opposite")
PER_PIECE = 1 + len(FLOW_NAMES) + len(SHARD_NAMES)
HALO = PER_PIECE * len(PIECES)
PER_HALO = LEVELS + 2
OUT = HALO + 4 * PER_HALO
PER_OUT = 3
X_SWAP = OUT + PER_OUT
X_NEAR = X_SWAP + 1
X_FORWARD = X_NEAR + X_CHUNKS
FLOWS = X_FORWARD + 2


def kernel(
    x_ref, wq_ref, wk_ref, wv_ref, out_ref,
    xbuf, wk, wv, wqa, wqb, khead, vhead, kbuf, vbuf, qbuf, stage, acc, top, total, cos_ref, sin_ref,
    send, recv, local,
):
    dp, seq = lax.axis_index("dp"), lax.axis_index("seq")
    hi, y, core = dp // 8, (dp // 2) % 4, dp % 2
    z, lo = seq // 2, seq % 2
    pick = (lo + hi) % 2
    up, down, across = (y + 1) % 4, (y + 3) % 4, (y + 2) % 4

    def device(hi, y, core, z, lo):
        return (hi * 8 + y * 2 + core, z * 2 + lo)

    partner = device(hi, y, 1 - core, z, lo)
    y_next, y_prev = device(hi, up, core, z, lo), device(hi, down, core, z, lo)
    x_far = device(1 - hi, y, core, z, 1 - lo)
    x_near = device(hi, y, core, z, 1 - lo)
    x_diag = device(hi, y, 1 - core, z, 1 - lo)
    z_next, z_prev = device(hi, y, core, (z + 1) % 8, lo), device(hi, y, core, (z + 7) % 8, lo)

    def remote(src, dst, flow, to):
        return pltpu.make_async_remote_copy(
            src_ref=src, dst_ref=dst, send_sem=send.at[flow], recv_sem=recv.at[flow],
            device_id=to, device_id_type=MESH,
        )

    def shard(g, yy):
        return g * 4 + yy

    def columns(name, c):
        if name == "k":
            return wk_ref.at[:, pl.ds(pl.multiple_of(c * 256, 256), 256)]
        if name == "v":
            return wv_ref.at[:, pl.ds(pl.multiple_of(c * 256, 256), 256)]
        first = (2 * c + pick) * 512 + (256 if name == "qb" else 0)
        return wq_ref.at[:, pl.ds(pl.multiple_of(first, 256), 256)]

    buffers = {"k": wk, "v": wv, "qa": wqa, "qb": wqb}
    mine = shard(hi, y)

    parity = z % 2

    class Piece:
        def __init__(self, name, along_z=None):
            self.index = PIECES.index(name)
            w = buffers[name]
            base = PER_PIECE * self.index

            def block(s, first, count, lanes):
                rows = pl.ds(pl.multiple_of(s * SHARD + first, 256), count)
                return w.at[rows, lanes]

            everything = pl.ds(0, 256)
            theirs = block(mine, core * 256, 256, everything)
            ours = block(mine, (1 - core) * 256, 256, everything)
            self.local = pltpu.make_async_copy(columns(name, core), theirs, local.at[self.index])
            self.swap_out = remote(columns(name, 1 - core), theirs, base, partner)
            self.swap_in = remote(ours, ours, base, partner)

            fetched, other = everything, None
            if along_z:
                fetched = pl.ds(pl.multiple_of(parity * 128, 128), 128)
                other = pl.ds(pl.multiple_of((1 - parity) * 128, 128), 128)

            def flow(name, to, out_shard, in_shard, part):
                number = base + 1 + FLOW_NAMES.index(name)
                out_part = block(out_shard, part * 256, 256, fetched)
                in_part = block(in_shard, part * 256, 256, fetched)
                return remote(out_part, out_part, number, to), remote(in_part, in_part, number, to)

            shards = {
                "below": shard(hi, down), "above": shard(hi, up), "opposite": shard(hi, across),
                "far": shard(1 - hi, y), "far_below": shard(1 - hi, down),
                "far_above": shard(1 - hi, up), "far_opposite": shard(1 - hi, across),
            }
            below, above, opposite, far, far_below, far_above, far_opposite = shards.values()
            self.flows = {
                "up_near": flow("up_near", y_next, below, opposite, 0),
                "down_near": flow("down_near", y_prev, above, opposite, 1),
            }
            for part in range(2):
                for name, to, out_shard, in_shard in (
                    ("up", y_next, mine, below),
                    ("down", y_prev, mine, above),
                    ("far", x_far, mine, far),
                    ("up_far", y_next, far, far_below),
                    ("down_far", y_prev, far, far_above),
                    ("far_across", x_far, opposite, far_opposite),
                ):
                    name += str(part)
                    self.flows[name] = flow(name, to, out_shard, in_shard, part)
            self.along = {}
            if along_z:
                for i, name in enumerate(SHARD_NAMES):
                    number = base + 1 + len(FLOW_NAMES) + i
                    to = z_next if name in along_z else z_prev
                    out_part = block(shards[name], 0, SHARD, fetched)
                    in_part = block(shards[name], 0, SHARD, other)
                    self.along[name] = (
                        remote(out_part, out_part, number, to), remote(in_part, in_part, number, to)
                    )

        def go(self, *flows):
            for f in flows:
                self.flows[f][0].start()

        def got(self, *flows):
            for f in flows:
                self.flows[f][1].wait_recv()

        def pass_on(self, *names):
            if self.along:
                for name in names:
                    self.along[name][0].start()

        def p0(self):
            self.local.wait()
            self.swap_in.wait_recv()
            self.go("up0", "down1", "far0", "far1", "up1", "down0")

        def p1(self):
            self.got("up0")
            self.go("up_near")
            self.got("down1")
            self.go("down_near")
            self.got("far0")
            self.go("up_far0", "down_far0")
            self.got("far1")
            self.go("up_far1", "down_far1")
            self.pass_on("far")

        def p2(self):
            self.got("up1")
            self.pass_on("below")
            self.got("down0")
            self.pass_on("above")
            self.got("up_near")
            self.go("far_across0")
            self.got("down_near")
            self.go("far_across1")
            self.pass_on("opposite")

        def p3(self):
            self.got("up_far0", "up_far1")
            self.pass_on("far_below")
            self.got("down_far0", "down_far1")
            self.pass_on("far_above")
            self.got("far_across0", "far_across1")
            self.pass_on("far_opposite")

        def p4(self):
            for _, landed in self.along.values():
                landed.wait_recv()

        def finish(self):
            self.swap_out.wait_send()
            for out, _ in [*self.flows.values(), *self.along.values()]:
                out.wait_send()

    k = Piece("k", along_z=("below", "above", "opposite"))
    v = Piece("v")
    qa = Piece("qa")
    qb = Piece("qb", along_z=("nothing",))
    pieces = (k, v, qa, qb)

    x_local = pltpu.make_async_copy(x_ref, xbuf.at[lo, core], local.at[4])
    for piece in pieces:
        piece.local.start()
    x_local.start()

    barrier = pltpu.get_barrier_semaphore()
    partners = (partner, y_next, y_prev, x_far, x_near, x_diag, z_next, z_prev)
    for other in partners:
        pl.semaphore_signal(barrier, inc=1, device_id=other, device_id_type=MESH)
    pl.semaphore_wait(barrier, len(partners))

    x_out = remote(x_ref, xbuf.at[lo, core], X_SWAP, partner)
    x_in = remote(xbuf.at[lo, 1 - core], xbuf.at[lo, 1 - core], X_SWAP, partner)

    def x_near_out(i):
        part = pl.ds(i * (SLAB // X_CHUNKS), SLAB // X_CHUNKS)
        return remote(x_ref.at[part], xbuf.at[lo, core, part], X_NEAR + i, x_near)

    def x_near_in(i):
        part = pl.ds(i * (SLAB // X_CHUNKS), SLAB // X_CHUNKS)
        there = xbuf.at[1 - lo, core, part]
        return remote(there, there, X_NEAR + i, x_near)

    def x_forward(piece, whose):
        there = xbuf.at[1 - lo, whose, pl.ds(piece * SLAB // 2, SLAB // 2)]
        return remote(there, there, X_FORWARD + piece, partner)

    def x_pass(piece):
        for i in range(piece * X_CHUNKS // 2, (piece + 1) * X_CHUNKS // 2):
            x_near_in(i).wait_recv()
        x_forward(piece, core).start()

    def x_got():
        for piece in range(2):
            x_forward(piece, 1 - core).wait_recv()

    for piece in pieces:
        piece.swap_out.start()
    x_out.start()

    def rope_tables():
        shape = (PAIR, HEAD_WIDTH)
        position = lax.broadcasted_iota(jnp.int32, shape, 0) + z * PAIR
        lane = lax.broadcasted_iota(jnp.int32, shape, 1)
        half = HEAD_WIDTH // 2
        exponent = (lane % half).astype(jnp.float32) * (-2.0 / HEAD_WIDTH)
        angle = position.astype(jnp.float32) * jnp.exp(exponent * LOG_ROPE_BASE)
        sine = jnp.sin(angle)
        cos_ref[...] = jnp.cos(angle).reshape(2, SLAB, HEAD_WIDTH)
        sin_ref[...] = jnp.where(lane < half, -sine, sine).reshape(2, SLAB, HEAD_WIDTH)

    def rotate(values, which):
        return values * cos_ref[which] + pltpu.roll(values, HEAD_WIDTH // 2, 1) * sin_ref[which]

    class Chain:
        def __init__(self, which, ctx, heads, buf):
            self.base = HALO + (2 * which + ctx) * PER_HALO
            self.ctx, self.heads, self.buf = ctx, heads, buf
            self.near_out = remote(
                heads.at[1 - pick, ctx], buf.at[0, ctx, lo], self.base + LEVELS, x_near
            )
            there = buf.at[0, ctx, 1 - lo]
            self.near_in = remote(there, there, self.base + LEVELS, x_near)

        def z_send(self, level):
            return remote(
                self.buf.at[level, self.ctx], self.buf.at[level + 1, self.ctx], self.base + level, z_next
            )

        def first_send(self, own):
            side = lo if own else 1 - lo
            number = self.base + (0 if own else LEVELS + 1)
            return remote(self.buf.at[0, self.ctx, side], self.buf.at[1, self.ctx, side], number, z_next)

        def open(self):
            self.buf[0, self.ctx, lo] = self.heads[pick, self.ctx]
            self.first_send(True).start()
            self.near_out.start()

        def level(self, level):
            if level == 0:
                self.near_in.wait_recv()
                self.first_send(False).start()
            elif level == 1:
                self.first_send(True).wait_recv()
                self.first_send(False).wait_recv()
            else:
                self.z_send(level - 1).wait_recv()
            if 0 < level < LEVELS:
                self.z_send(level).start()

        def finish(self):
            self.near_out.wait_send()
            self.first_send(True).wait_send()
            self.first_send(False).wait_send()
            for i in range(1, LEVELS):
                self.z_send(i).wait_send()

    k0, k1 = [Chain(0, ctx, khead, kbuf) for ctx in range(2)]
    v0, v1 = [Chain(1, ctx, vhead, vbuf) for ctx in range(2)]
    chains = (k0, k1, v0, v1)

    def project_k():
        @pl.loop(0, 2)
        def _(ctx):
            full = jnp.dot(xbuf[lo, ctx], wk[...], preferred_element_type=jnp.float32)
            for j in range(2):
                head = full[:, j * HEAD_WIDTH : (j + 1) * HEAD_WIDTH]
                khead[j, ctx] = rotate(head, lo).astype(jnp.bfloat16)

    def project_v():
        @pl.loop(0, 2)
        def _(ctx):
            full = jnp.dot(xbuf[lo, ctx], wv[...], preferred_element_type=jnp.float32)
            for j in range(2):
                vhead[j, ctx] = full[:, j * HEAD_WIDTH : (j + 1) * HEAD_WIDTH].astype(jnp.bfloat16)

    def project_q(half, w, side):
        @pl.loop(0, 2)
        def _(ctx):
            full = jnp.dot(xbuf[side, ctx], w[...], preferred_element_type=jnp.float32)
            for h in range(2):
                head = full[:, h * HEAD_WIDTH : (h + 1) * HEAD_WIDTH]
                qbuf[ctx, side, 2 * half + h] = rotate(head, side).astype(jnp.bfloat16)

    def scores(keys, ctx, side):
        queries = qbuf[ctx, side].reshape(TALL, HEAD_WIDTH)
        return lax.dot_general(
            keys, queries, (((1,), (1,)), ((), ())), preferred_element_type=jnp.float32
        )

    def weigh(values, p):
        return lax.dot_general(
            values, p.astype(jnp.bfloat16), (((0,), (0,)), ((), ())), preferred_element_type=jnp.float32
        )

    def visible(side, first_key, shape, newest):
        key = lax.broadcasted_iota(jnp.int32, shape, 0) + first_key
        token = lax.broadcasted_iota(jnp.int32, shape, 1) % SLAB + side * SLAB
        return key <= token if newest else key > token

    def begin(ctx, side):
        count = (side + 1) * SLAB
        keys = kbuf[0, ctx].reshape(PAIR, HEAD_WIDTH)[:count]
        values = vbuf[0, ctx].reshape(PAIR, HEAD_WIDTH)[:count]
        s = scores(keys, ctx, side)
        s = jnp.where(visible(side, 0, s.shape, True), s, negative_bound)
        m = jnp.max(s, axis=0, keepdims=True)
        p = jnp.exp2((s - m) * SCORE_SCALE)
        top[ctx, side] = m
        total[ctx, side] = jnp.sum(p, axis=0, keepdims=True)
        acc[ctx, side] = weigh(values, p)

    def update(ctx, side, s, values):
        old = top[ctx, side]
        m = jnp.maximum(old, jnp.max(s, axis=0, keepdims=True))
        factor = jnp.exp2((old - m) * SCORE_SCALE)
        p = jnp.exp2((s - m) * SCORE_SCALE)
        top[ctx, side] = m
        total[ctx, side] = total[ctx, side] * factor + jnp.sum(p, axis=0, keepdims=True)
        acc[ctx, side] = acc[ctx, side] * factor + weigh(values, p)

    def middle(ctx, side, level):
        keys = kbuf[level, ctx].reshape(PAIR, HEAD_WIDTH)
        values = vbuf[level, ctx].reshape(PAIR, HEAD_WIDTH)
        update(ctx, side, scores(keys, ctx, side), values)

    def oldest(ctx, side):
        first = side * SLAB
        keys = kbuf[LEVELS, ctx].reshape(PAIR, HEAD_WIDTH)[first:]
        values = vbuf[LEVELS, ctx].reshape(PAIR, HEAD_WIDTH)[first:]
        s = scores(keys, ctx, side)
        s = jnp.where(visible(side, first, s.shape, False), s, negative_bound)
        update(ctx, side, s, values)

    def attend(side, ctx, first, last):
        if first == 0:
            for static in range(2):
                pl.when(side == static)(functools.partial(begin, ctx, static))
        if last > 0:
            lax.fori_loop(
                max(first, 1), jnp.minimum(z, last) + 1,
                lambda level, c: (middle(ctx, side, level), c)[1], 0,
            )

    def conclude(ctx, side):
        for static in range(2):
            pl.when((z >= LEVELS) & (side == static))(functools.partial(oldest, ctx, static))
        result = (acc[ctx, side] / total[ctx, side]).T
        for h in range(GROUP):
            stage[side, ctx, :, h * HEAD_WIDTH : (h + 1) * HEAD_WIDTH] = result[
                h * SLAB : (h + 1) * SLAB
            ].astype(jnp.bfloat16)

    def out_columns(head):
        return out_ref.at[:, pl.ds(pl.multiple_of(head * 512, 512), 512)]

    head = 2 * core + pick

    def out_far(ctx):
        return remote(
            stage.at[1 - lo, ctx], out_columns(head), OUT + (ctx + core) % 2, device(hi, y, ctx, z, 1 - lo)
        )

    def out_partner():
        return remote(stage.at[lo, 1 - core], out_columns(head), OUT + 2, partner)

    def out_local():
        return pltpu.make_async_copy(stage.at[lo, core], out_columns(head), local.at[5])

    def close_far(ctx):
        conclude(ctx, 1 - lo)
        out_far(ctx).start()

    def close_own(ctx):
        conclude(ctx, lo)

        @pl.when(ctx == core)
        def _():
            out_local().start()

        @pl.when(ctx != core)
        def _():
            out_partner().start()

    def out_finish():
        out_local().wait()
        out_partner().wait_send()
        landed = out_columns(2 * (1 - core) + pick)
        remote(landed, landed, OUT + 2, partner).wait_recv()
        for other in range(2):
            out_far(other).wait_send()
            landed = out_columns(2 * ((core + other) % 2) + 1 - pick)
            remote(landed, landed, OUT + other, x_near).wait_recv()

    def x_go(*chunks):
        for i in chunks:
            x_near_out(i).start()

    k.p0()
    x_go(0, 1, 2)
    rope_tables()
    k.p1()
    k.p2()
    qb.p0()
    k.p3()
    qb.p1()
    x_local.wait()
    x_in.wait_recv()
    k.p4()
    project_k()
    k0.open()
    k1.open()
    x_go(3, 4)
    qb.p2()
    v.p0()
    k0.level(0)
    k1.level(0)
    qb.p3()
    v.p1()
    x_go(5)
    k0.level(1)
    k1.level(1)
    v.p2()
    qa.p0()
    k0.level(2)
    k1.level(2)
    v.p3()
    project_v()
    v0.open()
    v1.open()
    x_go(6, 7)
    qa.p1()
    k0.level(3)
    k1.level(3)
    v0.level(0)
    v1.level(0)
    qb.p4()
    project_q(1, wqb, lo)
    qa.p2()
    v0.level(1)
    k0.level(4)
    v1.level(1)
    k1.level(4)
    x_pass(0)
    qa.p3()
    project_q(0, wqa, lo)
    attend(lo, 0, 0, 1)
    v0.level(2)
    attend(lo, 1, 0, 1)
    x_pass(1)
    v1.level(2)
    attend(lo, 0, 2, 2)
    x_got()
    project_q(0, wqa, 1 - lo)
    v0.level(3)
    project_q(1, wqb, 1 - lo)
    attend(lo, 1, 2, 2)
    attend(1 - lo, 0, 0, 1)
    v1.level(3)
    attend(1 - lo, 0, 2, 3)
    attend(lo, 0, 3, 3)
    v0.level(4)
    close_far(0)
    attend(1 - lo, 1, 0, 3)
    attend(lo, 1, 3, 3)
    v1.level(4)
    close_far(1)
    close_own(0)
    close_own(1)

    for piece in pieces:
        piece.finish()
    x_out.wait_send()
    for i in range(X_CHUNKS):
        x_near_out(i).wait_send()
    for piece in range(2):
        x_forward(piece, core).wait_send()
    for chain in chains:
        chain.finish()
    out_finish()


def body(hidden_states, query_weight, key_matrix, value_matrix, context_lengths):
    x = hidden_states[0]
    seq = lax.axis_index("seq")
    any_space = pl.BlockSpec(memory_space=pl.ANY)
    bf16, f32 = jnp.bfloat16, jnp.float32
    attended = pl.pallas_call(
        kernel,
        out_shape=jax.ShapeDtypeStruct((SLAB, 2048), bf16),
        in_specs=[any_space] * 4,
        out_specs=any_space,
        scratch_shapes=[
            pltpu.VMEM((2, 2, SLAB, DEPTH), bf16),
            pltpu.VMEM((DEPTH, 256), bf16),
            pltpu.VMEM((DEPTH, 256), bf16),
            pltpu.VMEM((DEPTH, 256), bf16),
            pltpu.VMEM((DEPTH, 256), bf16),
            pltpu.VMEM((2, 2, SLAB, HEAD_WIDTH), bf16),
            pltpu.VMEM((2, 2, SLAB, HEAD_WIDTH), bf16),
            pltpu.VMEM((LEVELS + 1, 2, 2, SLAB, HEAD_WIDTH), bf16),
            pltpu.VMEM((LEVELS + 1, 2, 2, SLAB, HEAD_WIDTH), bf16),
            pltpu.VMEM((2, 2, GROUP, SLAB, HEAD_WIDTH), bf16),
            pltpu.VMEM((2, 2, SLAB, GROUP * HEAD_WIDTH), bf16),
            pltpu.VMEM((2, 2, HEAD_WIDTH, TALL), f32),
            pltpu.VMEM((2, 2, 1, TALL), f32),
            pltpu.VMEM((2, 2, 1, TALL), f32),
            pltpu.VMEM((2, SLAB, HEAD_WIDTH), f32),
            pltpu.VMEM((2, SLAB, HEAD_WIDTH), f32),
            pltpu.SemaphoreType.DMA((FLOWS,)),
            pltpu.SemaphoreType.DMA((FLOWS,)),
            pltpu.SemaphoreType.DMA((6,)),
        ],
        compiler_params=pltpu.CompilerParams(
            collective_id=0, has_side_effects=True, vmem_limit_bytes=56 * 2**20
        ),
        name="gather_project_attend",
    )(x, query_weight, key_matrix, value_matrix)
    positions = seq * SLAB + jnp.arange(SLAB, dtype=jnp.int32)
    valid = positions < context_lengths[0]
    return jnp.where(valid[:, None], attended, jnp.zeros_like(attended))[None]


def solution(mesh):
    return jax.shard_map(
        body,
        mesh=mesh,
        in_specs=(P("dp", "seq", None), P("dp", None), P("dp", None), P("dp", None), P("dp")),
        out_specs=P("dp", "seq", None),
        check_vma=False,
    )
```

```python
import functools

import jax
import jax.numpy as jnp
from jax import lax
from jax.experimental import pallas as pl
from jax.experimental.pallas import tpu as pltpu
from jax.sharding import PartitionSpec as P

HEAD_WIDTH = 128
SLAB = 256
PAIR = 2 * SLAB
SHARD = 512
SHARDS = 8
DEPTH = SHARD * SHARDS
LEVELS = 4
GROUP = 4
TALL = GROUP * SLAB
X_CHUNKS = 8
SCORE_SCALE = HEAD_WIDTH**-0.5 * 1.4426950408889634
LOG_ROPE_BASE = 9.210340371976184
negative_bound = -1e30
MESH = pl.DeviceIdType.MESH

PIECES = ("k", "v", "qa", "qb")
FLOW_NAMES = (
    "up0", "up1", "down1", "down0", "far0", "far1", "up_near", "down_near",
    "up_far0", "down_far0", "up_far1", "down_far1", "far_across0", "far_across1",
)
SHARD_NAMES = ("below", "above", "opposite", "far", "far_below", "far_above", "far_opposite")
PER_PIECE = 1 + len(FLOW_NAMES) + len(SHARD_NAMES)
HALO = PER_PIECE * len(PIECES)
PER_HALO = LEVELS + 2
OUT = HALO + 4 * PER_HALO
PER_OUT = 3
X_SWAP = OUT + PER_OUT
X_NEAR = X_SWAP + 1
X_FORWARD = X_NEAR + X_CHUNKS
BACK = X_FORWARD + 2
FLOWS = BACK + 4 * LEVELS


def kernel(
    x_ref, wq_ref, wk_ref, wv_ref, out_ref,
    xbuf, wk, wv, wqa, wqb, khead, vhead, kbuf, vbuf, kback, vback, qbuf, stage, acc, top, total, cos_ref, sin_ref,
    send, recv, local,
):
    dp, seq = lax.axis_index("dp"), lax.axis_index("seq")
    hi, y, core = dp // 8, (dp // 2) % 4, dp % 2
    z, lo = seq // 2, seq % 2
    pick = (lo + hi) % 2
    up, down, across = (y + 1) % 4, (y + 3) % 4, (y + 2) % 4

    def device(hi, y, core, z, lo):
        return (hi * 8 + y * 2 + core, z * 2 + lo)

    partner = device(hi, y, 1 - core, z, lo)
    y_next, y_prev = device(hi, up, core, z, lo), device(hi, down, core, z, lo)
    x_far = device(1 - hi, y, core, z, 1 - lo)
    x_near = device(hi, y, core, z, 1 - lo)
    x_diag = device(hi, y, 1 - core, z, 1 - lo)
    z_next, z_prev = device(hi, y, core, (z + 1) % 8, lo), device(hi, y, core, (z + 7) % 8, lo)

    def remote(src, dst, flow, to):
        return pltpu.make_async_remote_copy(
            src_ref=src, dst_ref=dst, send_sem=send.at[flow], recv_sem=recv.at[flow],
            device_id=to, device_id_type=MESH,
        )

    def shard(g, yy):
        return g * 4 + yy

    def columns(name, c):
        if name == "k":
            return wk_ref.at[:, pl.ds(pl.multiple_of(c * 256, 256), 256)]
        if name == "v":
            return wv_ref.at[:, pl.ds(pl.multiple_of(c * 256, 256), 256)]
        first = (2 * c + pick) * 512 + (256 if name == "qb" else 0)
        return wq_ref.at[:, pl.ds(pl.multiple_of(first, 256), 256)]

    buffers = {"k": wk, "v": wv, "qa": wqa, "qb": wqb}
    mine = shard(hi, y)

    parity = z % 2

    class Piece:
        def __init__(self, name, along_z=None):
            self.index = PIECES.index(name)
            w = buffers[name]
            base = PER_PIECE * self.index

            def block(s, first, count, lanes):
                rows = pl.ds(pl.multiple_of(s * SHARD + first, 256), count)
                return w.at[rows, lanes]

            everything = pl.ds(0, 256)
            theirs = block(mine, core * 256, 256, everything)
            ours = block(mine, (1 - core) * 256, 256, everything)
            self.local = pltpu.make_async_copy(columns(name, core), theirs, local.at[self.index])
            self.swap_out = remote(columns(name, 1 - core), theirs, base, partner)
            self.swap_in = remote(ours, ours, base, partner)

            fetched, other = everything, None
            if along_z:
                fetched = pl.ds(pl.multiple_of(parity * 128, 128), 128)
                other = pl.ds(pl.multiple_of((1 - parity) * 128, 128), 128)

            def flow(name, to, out_shard, in_shard, part):
                number = base + 1 + FLOW_NAMES.index(name)
                out_part = block(out_shard, part * 256, 256, fetched)
                in_part = block(in_shard, part * 256, 256, fetched)
                return remote(out_part, out_part, number, to), remote(in_part, in_part, number, to)

            shards = {
                "below": shard(hi, down), "above": shard(hi, up), "opposite": shard(hi, across),
                "far": shard(1 - hi, y), "far_below": shard(1 - hi, down),
                "far_above": shard(1 - hi, up), "far_opposite": shard(1 - hi, across),
            }
            below, above, opposite, far, far_below, far_above, far_opposite = shards.values()
            self.flows = {
                "up_near": flow("up_near", y_next, below, opposite, 0),
                "down_near": flow("down_near", y_prev, above, opposite, 1),
            }
            for part in range(2):
                for name, to, out_shard, in_shard in (
                    ("up", y_next, mine, below),
                    ("down", y_prev, mine, above),
                    ("far", x_far, mine, far),
                    ("up_far", y_next, far, far_below),
                    ("down_far", y_prev, far, far_above),
                    ("far_across", x_far, opposite, far_opposite),
                ):
                    name += str(part)
                    self.flows[name] = flow(name, to, out_shard, in_shard, part)
            self.along = {}
            if along_z:
                for i, name in enumerate(SHARD_NAMES):
                    number = base + 1 + len(FLOW_NAMES) + i
                    to = z_next if name in along_z else z_prev
                    out_part = block(shards[name], 0, SHARD, fetched)
                    in_part = block(shards[name], 0, SHARD, other)
                    self.along[name] = (
                        remote(out_part, out_part, number, to), remote(in_part, in_part, number, to)
                    )

        def go(self, *flows):
            for f in flows:
                self.flows[f][0].start()

        def got(self, *flows):
            for f in flows:
                self.flows[f][1].wait_recv()

        def pass_on(self, *names):
            if self.along:
                for name in names:
                    self.along[name][0].start()

        def p0(self):
            self.local.wait()
            self.swap_in.wait_recv()
            self.go("up0", "down1", "far0", "far1", "up1", "down0")

        def p1(self):
            self.got("up0")
            self.go("up_near")
            self.got("down1")
            self.go("down_near")
            self.got("far0")
            self.go("up_far0", "down_far0")
            self.got("far1")
            self.go("up_far1", "down_far1")
            self.pass_on("far")

        def p2(self):
            self.got("up1")
            self.pass_on("below")
            self.got("down0")
            self.pass_on("above")
            self.got("up_near")
            self.go("far_across0")
            self.got("down_near")
            self.go("far_across1")
            self.pass_on("opposite")

        def p3(self):
            self.got("up_far0", "up_far1")
            self.pass_on("far_below")
            self.got("down_far0", "down_far1")
            self.pass_on("far_above")
            self.got("far_across0", "far_across1")
            self.pass_on("far_opposite")

        def p4(self):
            for _, landed in self.along.values():
                landed.wait_recv()

        def finish(self):
            self.swap_out.wait_send()
            for out, _ in [*self.flows.values(), *self.along.values()]:
                out.wait_send()

    k = Piece("k", along_z=("below", "above", "opposite"))
    v = Piece("v")
    qa = Piece("qa")
    qb = Piece("qb", along_z=("nothing",))
    pieces = (k, v, qa, qb)

    x_local = pltpu.make_async_copy(x_ref, xbuf.at[lo, core], local.at[4])
    for piece in pieces:
        piece.local.start()
    x_local.start()

    barrier = pltpu.get_barrier_semaphore()
    partners = (partner, y_next, y_prev, x_far, x_near, x_diag, z_next, z_prev)
    for other in partners:
        pl.semaphore_signal(barrier, inc=1, device_id=other, device_id_type=MESH)
    pl.semaphore_wait(barrier, len(partners))

    x_out = remote(x_ref, xbuf.at[lo, core], X_SWAP, partner)
    x_in = remote(xbuf.at[lo, 1 - core], xbuf.at[lo, 1 - core], X_SWAP, partner)

    def x_near_out(i):
        part = pl.ds(i * (SLAB // X_CHUNKS), SLAB // X_CHUNKS)
        return remote(x_ref.at[part], xbuf.at[lo, core, part], X_NEAR + i, x_near)

    def x_near_in(i):
        part = pl.ds(i * (SLAB // X_CHUNKS), SLAB // X_CHUNKS)
        there = xbuf.at[1 - lo, core, part]
        return remote(there, there, X_NEAR + i, x_near)

    def x_forward(piece, whose):
        there = xbuf.at[1 - lo, whose, pl.ds(piece * SLAB // 2, SLAB // 2)]
        return remote(there, there, X_FORWARD + piece, partner)

    def x_pass(piece):
        for i in range(piece * X_CHUNKS // 2, (piece + 1) * X_CHUNKS // 2):
            x_near_in(i).wait_recv()
        x_forward(piece, core).start()

    def x_got():
        for piece in range(2):
            x_forward(piece, 1 - core).wait_recv()

    for piece in pieces:
        piece.swap_out.start()
    x_out.start()

    def rope_tables():
        shape = (PAIR, HEAD_WIDTH)
        position = lax.broadcasted_iota(jnp.int32, shape, 0) + z * PAIR
        lane = lax.broadcasted_iota(jnp.int32, shape, 1)
        half = HEAD_WIDTH // 2
        exponent = (lane % half).astype(jnp.float32) * (-2.0 / HEAD_WIDTH)
        angle = position.astype(jnp.float32) * jnp.exp(exponent * LOG_ROPE_BASE)
        sine = jnp.sin(angle)
        cos_ref[...] = jnp.cos(angle).reshape(2, SLAB, HEAD_WIDTH)
        sin_ref[...] = jnp.where(lane < half, -sine, sine).reshape(2, SLAB, HEAD_WIDTH)

    def rotate(values, which):
        return values * cos_ref[which] + pltpu.roll(values, HEAD_WIDTH // 2, 1) * sin_ref[which]

    class Chain:
        def __init__(self, which, turn, heads, buf):
            self.base = HALO + (2 * which + turn) * PER_HALO
            ctx = order[turn]
            self.ctx, self.heads, self.buf = ctx, heads, buf
            self.near_out = remote(
                heads.at[1 - pick, ctx], buf.at[0, ctx, lo], self.base + LEVELS, x_near
            )
            there = buf.at[0, ctx, 1 - lo]
            self.near_in = remote(there, there, self.base + LEVELS, x_near)

        def z_send(self, level):
            src, dst = self.buf.at[level, self.ctx], self.buf.at[level + 1, self.ctx]
            if level == LEVELS - 1:
                src, dst = src.at[1], dst.at[1]
            return remote(src, dst, self.base + level, z_next)

        def first_send(self, own):
            side = lo if own else 1 - lo
            number = self.base + (0 if own else LEVELS + 1)
            return remote(self.buf.at[0, self.ctx, side], self.buf.at[1, self.ctx, side], number, z_next)

        def near(self):
            self.near_out.start()

        def open(self, near=False):
            self.buf[0, self.ctx, lo] = self.heads[pick, self.ctx]
            self.first_send(True).start()
            if near:
                self.near()

        def level(self, level):
            if level == 0:
                self.near_in.wait_recv()
                self.first_send(False).start()
            elif level == 1:
                self.first_send(True).wait_recv()
                self.first_send(False).wait_recv()
            else:
                self.z_send(level - 1).wait_recv()
            if 0 < level < LEVELS:
                self.z_send(level).start()

        def finish(self):
            self.near_out.wait_send()
            self.first_send(True).wait_send()
            self.first_send(False).wait_send()
            for i in range(1, LEVELS):
                self.z_send(i).wait_send()

    class Back:
        def __init__(self, which, turn, buf, slots):
            self.base = BACK + (2 * which + turn) * LEVELS
            ctx = order[turn]
            between = [slots.at[i, ctx] for i in range(LEVELS - 1)]
            self.places = [buf.at[0, ctx, 0], *between, buf.at[LEVELS, ctx, 0]]

        def send(self, hop):
            return remote(self.places[hop], self.places[hop + 1], self.base + hop, z_prev)

        def hop(self, hop):
            if hop > 0:
                self.send(hop - 1).wait_recv()
            if hop < LEVELS:
                self.send(hop).start()

        def finish(self):
            for hop in range(LEVELS):
                self.send(hop).wait_send()

    order = (core, 1 - core)
    kb0, kb1 = [Back(0, turn, kbuf, kback) for turn in range(2)]
    vb0, vb1 = [Back(1, turn, vbuf, vback) for turn in range(2)]
    k0, k1 = [Chain(0, turn, khead, kbuf) for turn in range(2)]
    v0, v1 = [Chain(1, turn, vhead, vbuf) for turn in range(2)]
    chains = (k0, k1, v0, v1)

    def project_k():
        @pl.loop(0, 2)
        def _(ctx):
            full = jnp.dot(xbuf[lo, ctx], wk[...], preferred_element_type=jnp.float32)
            for j in range(2):
                head = full[:, j * HEAD_WIDTH : (j + 1) * HEAD_WIDTH]
                khead[j, ctx] = rotate(head, lo).astype(jnp.bfloat16)

    def project_v():
        @pl.loop(0, 2)
        def _(ctx):
            full = jnp.dot(xbuf[lo, ctx], wv[...], preferred_element_type=jnp.float32)
            for j in range(2):
                vhead[j, ctx] = full[:, j * HEAD_WIDTH : (j + 1) * HEAD_WIDTH].astype(jnp.bfloat16)

    def project_q(half, w, side, ctx):
        full = jnp.dot(xbuf[side, ctx], w[...], preferred_element_type=jnp.float32)
        for h in range(2):
            head = full[:, h * HEAD_WIDTH : (h + 1) * HEAD_WIDTH]
            qbuf[ctx, side, 2 * half + h] = rotate(head, side).astype(jnp.bfloat16)

    def project_side(side, ctx):
        project_q(0, wqa, side, ctx)
        project_q(1, wqb, side, ctx)

    def scores(keys, ctx, side):
        queries = qbuf[ctx, side].reshape(TALL, HEAD_WIDTH)
        return lax.dot_general(
            keys, queries, (((1,), (1,)), ((), ())), preferred_element_type=jnp.float32
        )

    def weigh(values, p):
        return lax.dot_general(
            values, p.astype(jnp.bfloat16), (((0,), (0,)), ((), ())), preferred_element_type=jnp.float32
        )

    def visible(side, first_key, shape, newest):
        key = lax.broadcasted_iota(jnp.int32, shape, 0) + first_key
        token = lax.broadcasted_iota(jnp.int32, shape, 1) % SLAB + side * SLAB
        return key <= token if newest else key > token

    def begin(ctx, side):
        count = (side + 1) * SLAB
        keys = kbuf[0, ctx].reshape(PAIR, HEAD_WIDTH)[:count]
        values = vbuf[0, ctx].reshape(PAIR, HEAD_WIDTH)[:count]
        s = scores(keys, ctx, side)
        s = jnp.where(visible(side, 0, s.shape, True), s, negative_bound)
        m = jnp.max(s, axis=0, keepdims=True)
        p = jnp.exp2((s - m) * SCORE_SCALE)
        top[ctx, side] = m
        total[ctx, side] = jnp.sum(p, axis=0, keepdims=True)
        acc[ctx, side] = weigh(values, p)

    def update(ctx, side, s, values):
        old = top[ctx, side]
        m = jnp.maximum(old, jnp.max(s, axis=0, keepdims=True))
        factor = jnp.exp2((old - m) * SCORE_SCALE)
        p = jnp.exp2((s - m) * SCORE_SCALE)
        top[ctx, side] = m
        total[ctx, side] = total[ctx, side] * factor + jnp.sum(p, axis=0, keepdims=True)
        acc[ctx, side] = acc[ctx, side] * factor + weigh(values, p)

    def middle(ctx, side, level):
        keys = kbuf[level, ctx].reshape(PAIR, HEAD_WIDTH)
        values = vbuf[level, ctx].reshape(PAIR, HEAD_WIDTH)
        update(ctx, side, scores(keys, ctx, side), values)

    def oldest(ctx, side):
        first = side * SLAB
        keys = kbuf[LEVELS, ctx].reshape(PAIR, HEAD_WIDTH)[first:]
        values = vbuf[LEVELS, ctx].reshape(PAIR, HEAD_WIDTH)[first:]
        s = scores(keys, ctx, side)
        s = jnp.where(visible(side, first, s.shape, False), s, negative_bound)
        update(ctx, side, s, values)

    def attend(side, ctx, first, last):
        if first == 0:
            for static in range(2):
                pl.when(side == static)(functools.partial(begin, ctx, static))
        if last > 0:
            lax.fori_loop(
                max(first, 1), jnp.minimum(z, last) + 1,
                lambda level, c: (middle(ctx, side, level), c)[1], 0,
            )

    def conclude(ctx, side):
        for static in range(2):
            pl.when((z >= LEVELS) & (side == static))(functools.partial(oldest, ctx, static))
        result = (acc[ctx, side] / total[ctx, side]).T
        for h in range(GROUP):
            stage[side, ctx, :, h * HEAD_WIDTH : (h + 1) * HEAD_WIDTH] = result[
                h * SLAB : (h + 1) * SLAB
            ].astype(jnp.bfloat16)

    def out_columns(head):
        return out_ref.at[:, pl.ds(pl.multiple_of(head * 512, 512), 512)]

    head = 2 * core + pick

    def out_far(turn):
        to = (x_near, x_diag)[turn]
        return remote(stage.at[1 - lo, order[turn]], out_columns(head), OUT + turn, to)

    def out_partner():
        return remote(stage.at[lo, 1 - core], out_columns(head), OUT + 2, partner)

    def out_local():
        return pltpu.make_async_copy(stage.at[lo, core], out_columns(head), local.at[5])

    def close_far(turn):
        conclude(order[turn], 1 - lo)
        out_far(turn).start()

    def close_own(turn):
        conclude(order[turn], lo)
        if turn == 0:
            out_local().start()
        else:
            out_partner().start()

    def out_finish():
        out_local().wait()
        out_partner().wait_send()
        landed = out_columns(2 * (1 - core) + pick)
        remote(landed, landed, OUT + 2, partner).wait_recv()
        for turn in range(2):
            out_far(turn).wait_send()
            landed = out_columns(2 * order[turn] + 1 - pick)
            remote(landed, landed, OUT + turn, x_near).wait_recv()

    first, second = order
    far = 1 - lo

    def x_go(*chunks):
        for i in chunks:
            x_near_out(i).start()

    k.p0()
    x_go(0, 1, 2)
    rope_tables()
    k.p1()
    k.p2()
    qb.p0()
    k.p3()
    qb.p1()
    x_local.wait()
    x_in.wait_recv()
    k.p4()
    project_k()
    k0.open(True)
    k1.open(True)
    x_go(3, 4)
    qb.p2()
    v.p0()
    k0.level(0)
    k1.level(0)
    kb0.hop(0)
    kb1.hop(0)
    qb.p3()
    v.p1()
    x_go(5)
    k0.level(1)
    k1.level(1)
    v.p2()
    qa.p0()
    k0.level(2)
    k1.level(2)
    kb0.hop(1)
    kb1.hop(1)
    v.p3()
    project_v()
    v0.open(True)
    v1.near()
    x_go(6, 7)
    k0.level(3)
    k1.level(3)
    qa.p1()
    v0.level(0)
    vb0.hop(0)
    kb0.hop(2)
    kb1.hop(2)
    qb.p4()
    project_q(1, wqb, lo, first)
    project_q(1, wqb, lo, second)
    v0.level(1)
    v1.open()
    v1.level(0)
    vb0.hop(1)
    vb1.hop(0)
    qa.p2()
    k0.level(4)
    k1.level(4)
    kb0.hop(3)
    kb1.hop(3)
    x_pass(0)
    qa.p3()
    project_q(0, wqa, lo, first)
    v0.level(2)
    vb0.hop(2)
    project_q(0, wqa, lo, second)
    v1.level(1)
    vb1.hop(1)
    attend(lo, first, 0, 1)
    x_pass(1)
    project_side(far, first)
    v0.level(3)
    attend(lo, first, 2, 2)
    vb0.hop(3)
    v1.level(2)
    vb1.hop(2)
    attend(far, first, 0, 3)
    kb0.hop(4)
    kb1.hop(4)
    vb0.hop(4)
    v0.level(4)
    close_far(0)
    v1.level(3)
    vb1.hop(3)
    x_got()
    project_side(far, second)
    attend(far, second, 0, 3)
    attend(lo, first, 3, 3)
    close_own(0)
    vb1.hop(4)
    v1.level(4)
    close_far(1)
    attend(lo, second, 0, 3)
    close_own(1)

    for piece in pieces:
        piece.finish()
    x_out.wait_send()
    for i in range(X_CHUNKS):
        x_near_out(i).wait_send()
    for piece in range(2):
        x_forward(piece, core).wait_send()
    for chain in (*chains, kb0, kb1, vb0, vb1):
        chain.finish()
    out_finish()


def body(hidden_states, query_weight, key_matrix, value_matrix, context_lengths):
    x = hidden_states[0]
    seq = lax.axis_index("seq")
    any_space = pl.BlockSpec(memory_space=pl.ANY)
    bf16, f32 = jnp.bfloat16, jnp.float32
    attended = pl.pallas_call(
        kernel,
        out_shape=jax.ShapeDtypeStruct((SLAB, 2048), bf16),
        in_specs=[any_space] * 4,
        out_specs=any_space,
        scratch_shapes=[
            pltpu.VMEM((2, 2, SLAB, DEPTH), bf16),
            pltpu.VMEM((DEPTH, 256), bf16),
            pltpu.VMEM((DEPTH, 256), bf16),
            pltpu.VMEM((DEPTH, 256), bf16),
            pltpu.VMEM((DEPTH, 256), bf16),
            pltpu.VMEM((2, 2, SLAB, HEAD_WIDTH), bf16),
            pltpu.VMEM((2, 2, SLAB, HEAD_WIDTH), bf16),
            pltpu.VMEM((LEVELS + 1, 2, 2, SLAB, HEAD_WIDTH), bf16),
            pltpu.VMEM((LEVELS + 1, 2, 2, SLAB, HEAD_WIDTH), bf16),
            pltpu.VMEM((LEVELS - 1, 2, SLAB, HEAD_WIDTH), bf16),
            pltpu.VMEM((LEVELS - 1, 2, SLAB, HEAD_WIDTH), bf16),
            pltpu.VMEM((2, 2, GROUP, SLAB, HEAD_WIDTH), bf16),
            pltpu.VMEM((2, 2, SLAB, GROUP * HEAD_WIDTH), bf16),
            pltpu.VMEM((2, 2, HEAD_WIDTH, TALL), f32),
            pltpu.VMEM((2, 2, 1, TALL), f32),
            pltpu.VMEM((2, 2, 1, TALL), f32),
            pltpu.VMEM((2, SLAB, HEAD_WIDTH), f32),
            pltpu.VMEM((2, SLAB, HEAD_WIDTH), f32),
            pltpu.SemaphoreType.DMA((FLOWS,)),
            pltpu.SemaphoreType.DMA((FLOWS,)),
            pltpu.SemaphoreType.DMA((6,)),
        ],
        compiler_params=pltpu.CompilerParams(
            collective_id=0, has_side_effects=True, vmem_limit_bytes=56 * 2**20
        ),
        name="gather_project_attend",
    )(x, query_weight, key_matrix, value_matrix)
    positions = seq * SLAB + jnp.arange(SLAB, dtype=jnp.int32)
    valid = positions < context_lengths[0]
    return jnp.where(valid[:, None], attended, jnp.zeros_like(attended))[None]


def solution(mesh):
    return jax.shard_map(
        body,
        mesh=mesh,
        in_specs=(P("dp", "seq", None), P("dp", None), P("dp", None), P("dp", None), P("dp")),
        out_specs=P("dp", "seq", None),
        check_vma=False,
    )
```

```python
import functools

import jax
import jax.numpy as jnp
from jax import lax
from jax.experimental import pallas as pl
from jax.experimental.pallas import tpu as pltpu
from jax.sharding import PartitionSpec as P

HEAD_WIDTH = 128
SLAB = 256
PAIR = 2 * SLAB
SHARD = 512
SHARDS = 8
DEPTH = SHARD * SHARDS
LEVELS = 4
GROUP = 4
TALL = GROUP * SLAB
X_CHUNKS = 8
SCORE_SCALE = HEAD_WIDTH**-0.5 * 1.4426950408889634
LOG_ROPE_BASE = 9.210340371976184
negative_bound = -1e30
MESH = pl.DeviceIdType.MESH

PIECES = ("k", "v", "qa", "qb")
FLOW_NAMES = (
    "up0", "up1", "down1", "down0", "far0", "far1", "up_near", "down_near",
    "up_far0", "down_far0", "up_far1", "down_far1", "far_across0", "far_across1",
)
SHARD_NAMES = ("below", "above", "opposite", "far", "far_below", "far_above", "far_opposite")
PER_PIECE = 1 + len(FLOW_NAMES) + len(SHARD_NAMES)
HALO = PER_PIECE * len(PIECES)
PER_HALO = LEVELS + 2
OUT = HALO + 4 * PER_HALO
PER_OUT = 3
X_SWAP = OUT + PER_OUT
X_NEAR = X_SWAP + 1
X_FORWARD = X_NEAR + X_CHUNKS
BACK = X_FORWARD + 2
FLOWS = BACK + 4 * LEVELS


def kernel(
    x_ref, wq_ref, wk_ref, wv_ref, out_ref,
    xbuf, wk, wv, wqa, wqb, khead, vhead, kbuf, vbuf, kback, vback, qbuf, stage, acc, top, total, cos_ref, sin_ref,
    send, recv, local,
):
    dp, seq = lax.axis_index("dp"), lax.axis_index("seq")
    hi, y, core = dp // 8, (dp // 2) % 4, dp % 2
    z, lo = seq // 2, seq % 2
    pick = (lo + hi) % 2
    up, down, across = (y + 1) % 4, (y + 3) % 4, (y + 2) % 4

    def device(hi, y, core, z, lo):
        return (hi * 8 + y * 2 + core, z * 2 + lo)

    partner = device(hi, y, 1 - core, z, lo)
    y_next, y_prev = device(hi, up, core, z, lo), device(hi, down, core, z, lo)
    x_far = device(1 - hi, y, core, z, 1 - lo)
    x_near = device(hi, y, core, z, 1 - lo)
    x_diag = device(hi, y, 1 - core, z, 1 - lo)
    z_next, z_prev = device(hi, y, core, (z + 1) % 8, lo), device(hi, y, core, (z + 7) % 8, lo)

    def remote(src, dst, flow, to):
        return pltpu.make_async_remote_copy(
            src_ref=src, dst_ref=dst, send_sem=send.at[flow], recv_sem=recv.at[flow],
            device_id=to, device_id_type=MESH,
        )

    def shard(g, yy):
        return g * 4 + yy

    def columns(name, c):
        if name == "k":
            return wk_ref.at[:, pl.ds(pl.multiple_of(c * 256, 256), 256)]
        if name == "v":
            return wv_ref.at[:, pl.ds(pl.multiple_of(c * 256, 256), 256)]
        first = (2 * c + pick) * 512 + (256 if name == "qb" else 0)
        return wq_ref.at[:, pl.ds(pl.multiple_of(first, 256), 256)]

    buffers = {"k": wk, "v": wv, "qa": wqa, "qb": wqb}
    mine = shard(hi, y)

    parity = z % 2

    class Piece:
        def __init__(self, name, along_z=None):
            self.index = PIECES.index(name)
            w = buffers[name]
            base = PER_PIECE * self.index

            def block(s, first, count, lanes):
                rows = pl.ds(pl.multiple_of(s * SHARD + first, 256), count)
                return w.at[rows, lanes]

            everything = pl.ds(0, 256)
            theirs = block(mine, core * 256, 256, everything)
            ours = block(mine, (1 - core) * 256, 256, everything)
            self.local = pltpu.make_async_copy(columns(name, core), theirs, local.at[self.index])
            self.swap_out = remote(columns(name, 1 - core), theirs, base, partner)
            self.swap_in = remote(ours, ours, base, partner)

            fetched, other = everything, None
            if along_z:
                fetched = pl.ds(pl.multiple_of(parity * 128, 128), 128)
                other = pl.ds(pl.multiple_of((1 - parity) * 128, 128), 128)

            def flow(name, to, out_shard, in_shard, part):
                number = base + 1 + FLOW_NAMES.index(name)
                out_part = block(out_shard, part * 256, 256, fetched)
                in_part = block(in_shard, part * 256, 256, fetched)
                return remote(out_part, out_part, number, to), remote(in_part, in_part, number, to)

            shards = {
                "below": shard(hi, down), "above": shard(hi, up), "opposite": shard(hi, across),
                "far": shard(1 - hi, y), "far_below": shard(1 - hi, down),
                "far_above": shard(1 - hi, up), "far_opposite": shard(1 - hi, across),
            }
            below, above, opposite, far, far_below, far_above, far_opposite = shards.values()
            self.flows = {
                "up_near": flow("up_near", y_next, below, opposite, 0),
                "down_near": flow("down_near", y_prev, above, opposite, 1),
            }
            for part in range(2):
                for name, to, out_shard, in_shard in (
                    ("up", y_next, mine, below),
                    ("down", y_prev, mine, above),
                    ("far", x_far, mine, far),
                    ("up_far", y_next, far, far_below),
                    ("down_far", y_prev, far, far_above),
                    ("far_across", x_far, opposite, far_opposite),
                ):
                    name += str(part)
                    self.flows[name] = flow(name, to, out_shard, in_shard, part)
            self.along = {}
            if along_z:
                for i, name in enumerate(SHARD_NAMES):
                    number = base + 1 + len(FLOW_NAMES) + i
                    to = z_next if name in along_z else z_prev
                    out_part = block(shards[name], 0, SHARD, fetched)
                    in_part = block(shards[name], 0, SHARD, other)
                    self.along[name] = (
                        remote(out_part, out_part, number, to), remote(in_part, in_part, number, to)
                    )

        def go(self, *flows):
            for f in flows:
                self.flows[f][0].start()

        def got(self, *flows):
            for f in flows:
                self.flows[f][1].wait_recv()

        def pass_on(self, *names):
            if self.along:
                for name in names:
                    self.along[name][0].start()

        def p0(self):
            self.local.wait()
            self.swap_in.wait_recv()
            self.go("up0", "down1", "far0", "far1", "up1", "down0")

        def p1(self):
            self.got("up0")
            self.go("up_near")
            self.got("down1")
            self.go("down_near")
            self.got("far0")
            self.go("up_far0", "down_far0")
            self.got("far1")
            self.go("up_far1", "down_far1")
            self.pass_on("far")

        def p2(self):
            self.got("up1")
            self.pass_on("below")
            self.got("down0")
            self.pass_on("above")
            self.got("up_near")
            self.go("far_across0")
            self.got("down_near")
            self.go("far_across1")
            self.pass_on("opposite")

        def p3(self):
            self.got("up_far0", "up_far1")
            self.pass_on("far_below")
            self.got("down_far0", "down_far1")
            self.pass_on("far_above")
            self.got("far_across0", "far_across1")
            self.pass_on("far_opposite")

        def p4(self):
            for _, landed in self.along.values():
                landed.wait_recv()

        def finish(self):
            self.swap_out.wait_send()
            for out, _ in [*self.flows.values(), *self.along.values()]:
                out.wait_send()

    k = Piece("k", along_z=("below", "above", "far_above", "far_opposite"))
    v = Piece("v")
    qa = Piece("qa")
    qb = Piece("qb", along_z=("nothing",))
    pieces = (k, v, qa, qb)

    x_local = pltpu.make_async_copy(x_ref, xbuf.at[lo, core], local.at[4])
    for piece in pieces:
        piece.local.start()
    x_local.start()

    barrier = pltpu.get_barrier_semaphore()
    partners = (partner, y_next, y_prev, x_far, x_near, x_diag, z_next, z_prev)
    for other in partners:
        pl.semaphore_signal(barrier, inc=1, device_id=other, device_id_type=MESH)
    pl.semaphore_wait(barrier, len(partners))

    x_out = remote(x_ref, xbuf.at[lo, core], X_SWAP, partner)
    x_in = remote(xbuf.at[lo, 1 - core], xbuf.at[lo, 1 - core], X_SWAP, partner)

    def x_near_out(i):
        part = pl.ds(i * (SLAB // X_CHUNKS), SLAB // X_CHUNKS)
        return remote(x_ref.at[part], xbuf.at[lo, core, part], X_NEAR + i, x_near)

    def x_near_in(i):
        part = pl.ds(i * (SLAB // X_CHUNKS), SLAB // X_CHUNKS)
        there = xbuf.at[1 - lo, core, part]
        return remote(there, there, X_NEAR + i, x_near)

    def x_forward(piece, whose):
        there = xbuf.at[1 - lo, whose, pl.ds(piece * SLAB // 2, SLAB // 2)]
        return remote(there, there, X_FORWARD + piece, partner)

    def x_pass(piece):
        for i in range(piece * X_CHUNKS // 2, (piece + 1) * X_CHUNKS // 2):
            x_near_in(i).wait_recv()
        x_forward(piece, core).start()

    def x_got():
        for piece in range(2):
            x_forward(piece, 1 - core).wait_recv()

    for piece in pieces:
        piece.swap_out.start()
    x_out.start()

    def rope_tables():
        shape = (PAIR, HEAD_WIDTH)
        position = lax.broadcasted_iota(jnp.int32, shape, 0) + z * PAIR
        lane = lax.broadcasted_iota(jnp.int32, shape, 1)
        half = HEAD_WIDTH // 2
        exponent = (lane % half).astype(jnp.float32) * (-2.0 / HEAD_WIDTH)
        angle = position.astype(jnp.float32) * jnp.exp(exponent * LOG_ROPE_BASE)
        sine = jnp.sin(angle)
        cos_ref[...] = jnp.cos(angle).reshape(2, SLAB, HEAD_WIDTH)
        sin_ref[...] = jnp.where(lane < half, -sine, sine).reshape(2, SLAB, HEAD_WIDTH)

    def rotate(values, which):
        return values * cos_ref[which] + pltpu.roll(values, HEAD_WIDTH // 2, 1) * sin_ref[which]

    class Chain:
        def __init__(self, which, turn, heads, buf):
            self.base = HALO + (2 * which + turn) * PER_HALO
            ctx = order[turn]
            self.ctx, self.heads, self.buf = ctx, heads, buf
            self.near_out = remote(
                heads.at[1 - pick, ctx], buf.at[0, ctx, lo], self.base + LEVELS, x_near
            )
            there = buf.at[0, ctx, 1 - lo]
            self.near_in = remote(there, there, self.base + LEVELS, x_near)

        def z_send(self, level):
            src, dst = self.buf.at[level, self.ctx], self.buf.at[level + 1, self.ctx]
            if level == LEVELS - 1:
                src, dst = src.at[1], dst.at[1]
            return remote(src, dst, self.base + level, z_next)

        def first_send(self, own):
            side = lo if own else 1 - lo
            number = self.base + (0 if own else LEVELS + 1)
            return remote(self.buf.at[0, self.ctx, side], self.buf.at[1, self.ctx, side], number, z_next)

        def near(self):
            self.near_out.start()

        def open(self, near=False):
            self.buf[0, self.ctx, lo] = self.heads[pick, self.ctx]
            self.first_send(True).start()
            if near:
                self.near()

        def level(self, level):
            if level == 0:
                self.near_in.wait_recv()
                self.first_send(False).start()
            elif level == 1:
                self.first_send(True).wait_recv()
                self.first_send(False).wait_recv()
            else:
                self.z_send(level - 1).wait_recv()
            if 0 < level < LEVELS:
                self.z_send(level).start()

        def finish(self):
            self.near_out.wait_send()
            self.first_send(True).wait_send()
            self.first_send(False).wait_send()
            for i in range(1, LEVELS):
                self.z_send(i).wait_send()

    class Back:
        def __init__(self, which, turn, buf, slots):
            self.base = BACK + (2 * which + turn) * LEVELS
            ctx = order[turn]
            between = [slots.at[i, ctx] for i in range(LEVELS - 1)]
            self.places = [buf.at[0, ctx, 0], *between, buf.at[LEVELS, ctx, 0]]

        def send(self, hop):
            return remote(self.places[hop], self.places[hop + 1], self.base + hop, z_prev)

        def hop(self, hop):
            if hop > 0:
                self.send(hop - 1).wait_recv()
            if hop < LEVELS:
                self.send(hop).start()

        def finish(self):
            for hop in range(LEVELS):
                self.send(hop).wait_send()

    order = (core, 1 - core)
    kb0, kb1 = [Back(0, turn, kbuf, kback) for turn in range(2)]
    vb0, vb1 = [Back(1, turn, vbuf, vback) for turn in range(2)]
    k0, k1 = [Chain(0, turn, khead, kbuf) for turn in range(2)]
    v0, v1 = [Chain(1, turn, vhead, vbuf) for turn in range(2)]
    chains = (k0, k1, v0, v1)

    def project_k():
        @pl.loop(0, 2)
        def _(ctx):
            full = jnp.dot(xbuf[lo, ctx], wk[...], preferred_element_type=jnp.float32)
            for j in range(2):
                head = full[:, j * HEAD_WIDTH : (j + 1) * HEAD_WIDTH]
                khead[j, ctx] = rotate(head, lo).astype(jnp.bfloat16)

    def project_v():
        @pl.loop(0, 2)
        def _(ctx):
            full = jnp.dot(xbuf[lo, ctx], wv[...], preferred_element_type=jnp.float32)
            for j in range(2):
                vhead[j, ctx] = full[:, j * HEAD_WIDTH : (j + 1) * HEAD_WIDTH].astype(jnp.bfloat16)

    def project_q(half, w, side, ctx):
        full = jnp.dot(xbuf[side, ctx], w[...], preferred_element_type=jnp.float32)
        for h in range(2):
            head = full[:, h * HEAD_WIDTH : (h + 1) * HEAD_WIDTH]
            qbuf[ctx, side, 2 * half + h] = rotate(head, side).astype(jnp.bfloat16)

    def project_side(side, ctx):
        project_q(0, wqa, side, ctx)
        project_q(1, wqb, side, ctx)

    def scores(keys, ctx, side):
        queries = qbuf[ctx, side].reshape(TALL, HEAD_WIDTH)
        return lax.dot_general(
            keys, queries, (((1,), (1,)), ((), ())), preferred_element_type=jnp.float32
        )

    def weigh(values, p):
        return lax.dot_general(
            values, p.astype(jnp.bfloat16), (((0,), (0,)), ((), ())), preferred_element_type=jnp.float32
        )

    def visible(side, first_key, shape, newest):
        key = lax.broadcasted_iota(jnp.int32, shape, 0) + first_key
        token = lax.broadcasted_iota(jnp.int32, shape, 1) % SLAB + side * SLAB
        return key <= token if newest else key > token

    def begin(ctx, side):
        count = (side + 1) * SLAB
        keys = kbuf[0, ctx].reshape(PAIR, HEAD_WIDTH)[:count]
        values = vbuf[0, ctx].reshape(PAIR, HEAD_WIDTH)[:count]
        s = scores(keys, ctx, side)
        s = jnp.where(visible(side, 0, s.shape, True), s, negative_bound)
        m = jnp.max(s, axis=0, keepdims=True)
        p = jnp.exp2((s - m) * SCORE_SCALE)
        top[ctx, side] = m
        total[ctx, side] = jnp.sum(p, axis=0, keepdims=True)
        acc[ctx, side] = weigh(values, p)

    def update(ctx, side, s, values):
        old = top[ctx, side]
        m = jnp.maximum(old, jnp.max(s, axis=0, keepdims=True))
        factor = jnp.exp2((old - m) * SCORE_SCALE)
        p = jnp.exp2((s - m) * SCORE_SCALE)
        top[ctx, side] = m
        total[ctx, side] = total[ctx, side] * factor + jnp.sum(p, axis=0, keepdims=True)
        acc[ctx, side] = acc[ctx, side] * factor + weigh(values, p)

    def middle(ctx, side, level):
        keys = kbuf[level, ctx].reshape(PAIR, HEAD_WIDTH)
        values = vbuf[level, ctx].reshape(PAIR, HEAD_WIDTH)
        update(ctx, side, scores(keys, ctx, side), values)

    def oldest(ctx, side):
        first = side * SLAB
        keys = kbuf[LEVELS, ctx].reshape(PAIR, HEAD_WIDTH)[first:]
        values = vbuf[LEVELS, ctx].reshape(PAIR, HEAD_WIDTH)[first:]
        s = scores(keys, ctx, side)
        s = jnp.where(visible(side, first, s.shape, False), s, negative_bound)
        update(ctx, side, s, values)

    def attend(side, ctx, first, last):
        if first == 0:
            for static in range(2):
                pl.when(side == static)(functools.partial(begin, ctx, static))
        if last > 0:
            lax.fori_loop(
                max(first, 1), jnp.minimum(z, last) + 1,
                lambda level, c: (middle(ctx, side, level), c)[1], 0,
            )

    def conclude(ctx, side):
        for static in range(2):
            pl.when((z >= LEVELS) & (side == static))(functools.partial(oldest, ctx, static))
        result = (acc[ctx, side] / total[ctx, side]).T
        for h in range(GROUP):
            stage[side, ctx, :, h * HEAD_WIDTH : (h + 1) * HEAD_WIDTH] = result[
                h * SLAB : (h + 1) * SLAB
            ].astype(jnp.bfloat16)

    def out_columns(head):
        return out_ref.at[:, pl.ds(pl.multiple_of(head * 512, 512), 512)]

    head = 2 * core + pick

    def out_far(turn):
        to = (x_near, x_diag)[turn]
        return remote(stage.at[1 - lo, order[turn]], out_columns(head), OUT + turn, to)

    def out_partner():
        return remote(stage.at[lo, 1 - core], out_columns(head), OUT + 2, partner)

    def out_local():
        return pltpu.make_async_copy(stage.at[lo, core], out_columns(head), local.at[5])

    def close_far(turn):
        conclude(order[turn], 1 - lo)
        out_far(turn).start()

    def close_own(turn):
        conclude(order[turn], lo)
        if turn == 0:
            out_local().start()
        else:
            out_partner().start()

    def out_finish():
        out_local().wait()
        out_partner().wait_send()
        landed = out_columns(2 * (1 - core) + pick)
        remote(landed, landed, OUT + 2, partner).wait_recv()
        for turn in range(2):
            out_far(turn).wait_send()
            landed = out_columns(2 * order[turn] + 1 - pick)
            remote(landed, landed, OUT + turn, x_near).wait_recv()

    first, second = order
    far = 1 - lo

    def x_go(*chunks):
        for i in chunks:
            x_near_out(i).start()

    k.p0()
    x_go(0, 1, 2)
    rope_tables()
    k.p1()
    k.p2()
    qb.p0()
    k.p3()
    qb.p1()
    x_local.wait()
    x_in.wait_recv()
    k.p4()
    project_k()
    k0.open(True)
    k1.open(True)
    x_go(3, 4)
    qb.p2()
    v.p0()
    k0.level(0)
    k1.level(0)
    kb0.hop(0)
    kb1.hop(0)
    qb.p3()
    v.p1()
    x_go(5)
    k0.level(1)
    k1.level(1)
    v.p2()
    qa.p0()
    k0.level(2)
    k1.level(2)
    kb0.hop(1)
    kb1.hop(1)
    v.p3()
    project_v()
    v0.open(True)
    v1.open(True)
    x_go(6, 7)
    k0.level(3)
    k1.level(3)
    qa.p1()
    v0.level(0)
    v1.level(0)
    vb0.hop(0)
    vb1.hop(0)
    kb0.hop(2)
    kb1.hop(2)
    qb.p4()
    project_q(1, wqb, lo, first)
    project_q(1, wqb, lo, second)
    qa.p2()
    v0.level(1)
    v1.level(1)
    vb0.hop(1)
    vb1.hop(1)
    k0.level(4)
    k1.level(4)
    kb0.hop(3)
    kb1.hop(3)
    x_pass(0)
    qa.p3()
    project_q(0, wqa, lo, first)
    project_q(0, wqa, lo, second)
    attend(lo, first, 0, 1)
    v0.level(2)
    vb0.hop(2)
    attend(lo, second, 0, 1)
    v1.level(2)
    vb1.hop(2)
    x_pass(1)
    project_side(far, first)
    attend(far, first, 0, 1)
    v0.level(3)
    vb0.hop(3)
    attend(far, first, 2, 2)
    v1.level(3)
    vb1.hop(3)
    attend(far, first, 3, 3)
    kb0.hop(4)
    kb1.hop(4)
    vb0.hop(4)
    v0.level(4)
    close_far(0)
    x_got()
    project_side(far, second)
    attend(far, second, 0, 3)
    vb1.hop(4)
    v1.level(4)
    close_far(1)
    attend(lo, first, 2, 3)
    close_own(0)
    attend(lo, second, 2, 3)
    close_own(1)

    for piece in pieces:
        piece.finish()
    x_out.wait_send()
    for i in range(X_CHUNKS):
        x_near_out(i).wait_send()
    for piece in range(2):
        x_forward(piece, core).wait_send()
    for chain in (*chains, kb0, kb1, vb0, vb1):
        chain.finish()
    out_finish()


def body(hidden_states, query_weight, key_matrix, value_matrix, context_lengths):
    x = hidden_states[0]
    seq = lax.axis_index("seq")
    any_space = pl.BlockSpec(memory_space=pl.ANY)
    bf16, f32 = jnp.bfloat16, jnp.float32
    attended = pl.pallas_call(
        kernel,
        out_shape=jax.ShapeDtypeStruct((SLAB, 2048), bf16),
        in_specs=[any_space] * 4,
        out_specs=any_space,
        scratch_shapes=[
            pltpu.VMEM((2, 2, SLAB, DEPTH), bf16),
            pltpu.VMEM((DEPTH, 256), bf16),
            pltpu.VMEM((DEPTH, 256), bf16),
            pltpu.VMEM((DEPTH, 256), bf16),
            pltpu.VMEM((DEPTH, 256), bf16),
            pltpu.VMEM((2, 2, SLAB, HEAD_WIDTH), bf16),
            pltpu.VMEM((2, 2, SLAB, HEAD_WIDTH), bf16),
            pltpu.VMEM((LEVELS + 1, 2, 2, SLAB, HEAD_WIDTH), bf16),
            pltpu.VMEM((LEVELS + 1, 2, 2, SLAB, HEAD_WIDTH), bf16),
            pltpu.VMEM((LEVELS - 1, 2, SLAB, HEAD_WIDTH), bf16),
            pltpu.VMEM((LEVELS - 1, 2, SLAB, HEAD_WIDTH), bf16),
            pltpu.VMEM((2, 2, GROUP, SLAB, HEAD_WIDTH), bf16),
            pltpu.VMEM((2, 2, SLAB, GROUP * HEAD_WIDTH), bf16),
            pltpu.VMEM((2, 2, HEAD_WIDTH, TALL), f32),
            pltpu.VMEM((2, 2, 1, TALL), f32),
            pltpu.VMEM((2, 2, 1, TALL), f32),
            pltpu.VMEM((2, SLAB, HEAD_WIDTH), f32),
            pltpu.VMEM((2, SLAB, HEAD_WIDTH), f32),
            pltpu.SemaphoreType.DMA((FLOWS,)),
            pltpu.SemaphoreType.DMA((FLOWS,)),
            pltpu.SemaphoreType.DMA((6,)),
        ],
        compiler_params=pltpu.CompilerParams(
            collective_id=0, has_side_effects=True, vmem_limit_bytes=56 * 2**20
        ),
        name="gather_project_attend",
    )(x, query_weight, key_matrix, value_matrix)
    positions = seq * SLAB + jnp.arange(SLAB, dtype=jnp.int32)
    valid = positions < context_lengths[0]
    return jnp.where(valid[:, None], attended, jnp.zeros_like(attended))[None]


def solution(mesh):
    return jax.shard_map(
        body,
        mesh=mesh,
        in_specs=(P("dp", "seq", None), P("dp", None), P("dp", None), P("dp", None), P("dp")),
        out_specs=P("dp", "seq", None),
        check_vma=False,
    )
```

```python
import functools

import jax
import jax.numpy as jnp
from jax import lax
from jax.experimental import pallas as pl
from jax.experimental.pallas import tpu as pltpu
from jax.sharding import PartitionSpec as P

HEAD_WIDTH = 128
SLAB = 256
PAIR = 2 * SLAB
SHARD = 512
SHARDS = 8
DEPTH = SHARD * SHARDS
LEVELS = 4
GROUP = 4
TALL = GROUP * SLAB
X_CHUNKS = 8
SCORE_SCALE = HEAD_WIDTH**-0.5 * 1.4426950408889634
LOG_ROPE_BASE = 9.210340371976184
negative_bound = -1e30
MESH = pl.DeviceIdType.MESH

PIECES = ("k", "v", "qa", "qb")
FLOW_NAMES = (
    "up0", "up1", "down1", "down0", "far0", "far1", "up_near", "down_near",
    "up_far0", "down_far0", "up_far1", "down_far1", "far_across0", "far_across1",
)
SHARD_NAMES = ("below", "above", "opposite", "far", "far_below", "far_above", "far_opposite")
PER_PIECE = 1 + len(FLOW_NAMES) + len(SHARD_NAMES)
HALO = PER_PIECE * len(PIECES)
PER_HALO = LEVELS + 2
OUT = HALO + 4 * PER_HALO
PER_OUT = 3
X_SWAP = OUT + PER_OUT
X_NEAR = X_SWAP + 1
X_FORWARD = X_NEAR + X_CHUNKS
BACK = X_FORWARD + 2
FLOWS = BACK + 4 * LEVELS


def kernel(
    x_ref, wq_ref, wk_ref, wv_ref, out_ref,
    xbuf, wk, wv, wqa, wqb, khead, vhead, kbuf, vbuf, kback, vback, qbuf, stage, acc, top, total, cos_ref, sin_ref,
    send, recv, local,
):
    dp, seq = lax.axis_index("dp"), lax.axis_index("seq")
    hi, y, core = dp // 8, (dp // 2) % 4, dp % 2
    z, lo = seq // 2, seq % 2
    pick = (lo + hi) % 2
    up, down, across = (y + 1) % 4, (y + 3) % 4, (y + 2) % 4

    def device(hi, y, core, z, lo):
        return (hi * 8 + y * 2 + core, z * 2 + lo)

    partner = device(hi, y, 1 - core, z, lo)
    y_next, y_prev = device(hi, up, core, z, lo), device(hi, down, core, z, lo)
    x_far = device(1 - hi, y, core, z, 1 - lo)
    x_near = device(hi, y, core, z, 1 - lo)
    x_diag = device(hi, y, 1 - core, z, 1 - lo)
    z_next, z_prev = device(hi, y, core, (z + 1) % 8, lo), device(hi, y, core, (z + 7) % 8, lo)

    def remote(src, dst, flow, to):
        return pltpu.make_async_remote_copy(
            src_ref=src, dst_ref=dst, send_sem=send.at[flow], recv_sem=recv.at[flow],
            device_id=to, device_id_type=MESH,
        )

    def shard(g, yy):
        return g * 4 + yy

    def columns(name, c):
        if name == "k":
            return wk_ref.at[:, pl.ds(pl.multiple_of(c * 256, 256), 256)]
        if name == "v":
            return wv_ref.at[:, pl.ds(pl.multiple_of(c * 256, 256), 256)]
        first = (2 * c + pick) * 512 + (256 if name == "qb" else 0)
        return wq_ref.at[:, pl.ds(pl.multiple_of(first, 256), 256)]

    buffers = {"k": wk, "v": wv, "qa": wqa, "qb": wqb}
    mine = shard(hi, y)

    parity = z % 2

    class Piece:
        def __init__(self, name, along_z=None):
            self.index = PIECES.index(name)
            w = buffers[name]
            base = PER_PIECE * self.index

            def block(s, first, count, lanes):
                rows = pl.ds(pl.multiple_of(s * SHARD + first, 256), count)
                return w.at[rows, lanes]

            everything = pl.ds(0, 256)
            theirs = block(mine, core * 256, 256, everything)
            ours = block(mine, (1 - core) * 256, 256, everything)
            self.local = pltpu.make_async_copy(columns(name, core), theirs, local.at[self.index])
            self.swap_out = remote(columns(name, 1 - core), theirs, base, partner)
            self.swap_in = remote(ours, ours, base, partner)

            fetched, other = everything, None
            if along_z:
                fetched = pl.ds(pl.multiple_of(parity * 128, 128), 128)
                other = pl.ds(pl.multiple_of((1 - parity) * 128, 128), 128)

            def flow(name, to, out_shard, in_shard, part):
                number = base + 1 + FLOW_NAMES.index(name)
                out_part = block(out_shard, part * 256, 256, fetched)
                in_part = block(in_shard, part * 256, 256, fetched)
                return remote(out_part, out_part, number, to), remote(in_part, in_part, number, to)

            shards = {
                "below": shard(hi, down), "above": shard(hi, up), "opposite": shard(hi, across),
                "far": shard(1 - hi, y), "far_below": shard(1 - hi, down),
                "far_above": shard(1 - hi, up), "far_opposite": shard(1 - hi, across),
            }
            below, above, opposite, far, far_below, far_above, far_opposite = shards.values()
            self.flows = {
                "up_near": flow("up_near", y_next, below, opposite, 0),
                "down_near": flow("down_near", y_prev, above, opposite, 1),
            }
            for part in range(2):
                for name, to, out_shard, in_shard in (
                    ("up", y_next, mine, below),
                    ("down", y_prev, mine, above),
                    ("far", x_far, mine, far),
                    ("up_far", y_next, far, far_below),
                    ("down_far", y_prev, far, far_above),
                    ("far_across", x_far, opposite, far_opposite),
                ):
                    name += str(part)
                    self.flows[name] = flow(name, to, out_shard, in_shard, part)
            self.along = {}
            if along_z:
                for i, name in enumerate(SHARD_NAMES):
                    number = base + 1 + len(FLOW_NAMES) + i
                    to = z_next if name in along_z else z_prev
                    out_part = block(shards[name], 0, SHARD, fetched)
                    in_part = block(shards[name], 0, SHARD, other)
                    self.along[name] = (
                        remote(out_part, out_part, number, to), remote(in_part, in_part, number, to)
                    )

        def go(self, *flows):
            for f in flows:
                self.flows[f][0].start()

        def got(self, *flows):
            for f in flows:
                self.flows[f][1].wait_recv()

        def pass_on(self, *names):
            if self.along:
                for name in names:
                    self.along[name][0].start()

        def p0(self):
            self.local.wait()
            self.swap_in.wait_recv()
            self.go("up0", "down1", "far0", "far1", "up1", "down0")

        def p1(self):
            self.got("up0")
            self.go("up_near")
            self.got("down1")
            self.go("down_near")
            self.got("far0")
            self.go("up_far0", "down_far0")
            self.got("far1")
            self.go("up_far1", "down_far1")
            self.pass_on("far")

        def p2(self):
            self.got("up1")
            self.pass_on("below")
            self.got("down0")
            self.pass_on("above")
            self.got("up_near")
            self.go("far_across0")
            self.got("down_near")
            self.go("far_across1")
            self.pass_on("opposite")

        def p3(self):
            self.got("up_far0", "up_far1")
            self.pass_on("far_below")
            self.got("down_far0", "down_far1")
            self.pass_on("far_above")
            self.got("far_across0", "far_across1")
            self.pass_on("far_opposite")

        def p4(self):
            for _, landed in self.along.values():
                landed.wait_recv()

        def finish(self):
            self.swap_out.wait_send()
            for out, _ in [*self.flows.values(), *self.along.values()]:
                out.wait_send()

    k = Piece("k", along_z=("below", "above", "far_above", "far_opposite"))
    v = Piece("v")
    qa = Piece("qa")
    qb = Piece("qb", along_z=("nothing",))
    pieces = (k, v, qa, qb)

    x_local = pltpu.make_async_copy(x_ref, xbuf.at[lo, core], local.at[4])
    for piece in pieces:
        piece.local.start()
    x_local.start()

    barrier = pltpu.get_barrier_semaphore()
    partners = (partner, y_next, y_prev, x_far, x_near, x_diag, z_next, z_prev)
    for other in partners:
        pl.semaphore_signal(barrier, inc=1, device_id=other, device_id_type=MESH)
    pl.semaphore_wait(barrier, len(partners))

    x_out = remote(x_ref, xbuf.at[lo, core], X_SWAP, partner)
    x_in = remote(xbuf.at[lo, 1 - core], xbuf.at[lo, 1 - core], X_SWAP, partner)

    def x_near_out(i):
        part = pl.ds(i * (SLAB // X_CHUNKS), SLAB // X_CHUNKS)
        return remote(x_ref.at[part], xbuf.at[lo, core, part], X_NEAR + i, x_near)

    def x_near_in(i):
        part = pl.ds(i * (SLAB // X_CHUNKS), SLAB // X_CHUNKS)
        there = xbuf.at[1 - lo, core, part]
        return remote(there, there, X_NEAR + i, x_near)

    def x_forward(piece, whose):
        there = xbuf.at[1 - lo, whose, pl.ds(piece * SLAB // 2, SLAB // 2)]
        return remote(there, there, X_FORWARD + piece, partner)

    def x_pass(piece):
        for i in range(piece * X_CHUNKS // 2, (piece + 1) * X_CHUNKS // 2):
            x_near_in(i).wait_recv()
        x_forward(piece, core).start()

    def x_got():
        for piece in range(2):
            x_forward(piece, 1 - core).wait_recv()

    for piece in pieces:
        piece.swap_out.start()
    x_out.start()

    def rope_tables():
        shape = (PAIR, HEAD_WIDTH)
        position = lax.broadcasted_iota(jnp.int32, shape, 0) + z * PAIR
        lane = lax.broadcasted_iota(jnp.int32, shape, 1)
        half = HEAD_WIDTH // 2
        exponent = (lane % half).astype(jnp.float32) * (-2.0 / HEAD_WIDTH)
        angle = position.astype(jnp.float32) * jnp.exp(exponent * LOG_ROPE_BASE)
        sine = jnp.sin(angle)
        cos_ref[...] = jnp.cos(angle).reshape(2, SLAB, HEAD_WIDTH)
        sin_ref[...] = jnp.where(lane < half, -sine, sine).reshape(2, SLAB, HEAD_WIDTH)

    def rotate(values, which):
        return values * cos_ref[which] + pltpu.roll(values, HEAD_WIDTH // 2, 1) * sin_ref[which]

    class Chain:
        def __init__(self, which, turn, heads, buf):
            self.base = HALO + (2 * which + turn) * PER_HALO
            ctx = order[turn]
            self.ctx, self.heads, self.buf = ctx, heads, buf
            self.near_out = remote(
                heads.at[1 - pick, ctx], buf.at[0, ctx, lo], self.base + LEVELS, x_near
            )
            there = buf.at[0, ctx, 1 - lo]
            self.near_in = remote(there, there, self.base + LEVELS, x_near)

        def z_send(self, level):
            src, dst = self.buf.at[level, self.ctx], self.buf.at[level + 1, self.ctx]
            if level == LEVELS - 1:
                src, dst = src.at[1], dst.at[1]
            return remote(src, dst, self.base + level, z_next)

        def first_send(self, own):
            side = lo if own else 1 - lo
            number = self.base + (0 if own else LEVELS + 1)
            return remote(self.buf.at[0, self.ctx, side], self.buf.at[1, self.ctx, side], number, z_next)

        def near(self):
            self.near_out.start()

        def open(self, near=False):
            self.buf[0, self.ctx, lo] = self.heads[pick, self.ctx]
            self.first_send(True).start()
            if near:
                self.near()

        def level(self, level):
            if level == 0:
                self.near_in.wait_recv()
                self.first_send(False).start()
            elif level == 1:
                self.first_send(True).wait_recv()
                self.first_send(False).wait_recv()
            else:
                self.z_send(level - 1).wait_recv()
            if 0 < level < LEVELS:
                self.z_send(level).start()

        def finish(self):
            self.near_out.wait_send()
            self.first_send(True).wait_send()
            self.first_send(False).wait_send()
            for i in range(1, LEVELS):
                self.z_send(i).wait_send()

    class Back:
        def __init__(self, which, turn, buf, slots):
            self.base = BACK + (2 * which + turn) * LEVELS
            ctx = order[turn]
            between = [slots.at[i, ctx] for i in range(LEVELS - 1)]
            self.places = [buf.at[0, ctx, 0], *between, buf.at[LEVELS, ctx, 0]]

        def send(self, hop):
            return remote(self.places[hop], self.places[hop + 1], self.base + hop, z_prev)

        def hop(self, hop):
            if hop > 0:
                self.send(hop - 1).wait_recv()
            if hop < LEVELS:
                self.send(hop).start()

        def finish(self):
            for hop in range(LEVELS):
                self.send(hop).wait_send()

    order = (core, 1 - core)
    kb0, kb1 = [Back(0, turn, kbuf, kback) for turn in range(2)]
    vb0, vb1 = [Back(1, turn, vbuf, vback) for turn in range(2)]
    k0, k1 = [Chain(0, turn, khead, kbuf) for turn in range(2)]
    v0, v1 = [Chain(1, turn, vhead, vbuf) for turn in range(2)]
    chains = (k0, k1, v0, v1)

    def project_k():
        @pl.loop(0, 2)
        def _(ctx):
            full = jnp.dot(xbuf[lo, ctx], wk[...], preferred_element_type=jnp.float32)
            for j in range(2):
                head = full[:, j * HEAD_WIDTH : (j + 1) * HEAD_WIDTH]
                khead[j, ctx] = rotate(head, lo).astype(jnp.bfloat16)

    def project_v():
        @pl.loop(0, 2)
        def _(ctx):
            full = jnp.dot(xbuf[lo, ctx], wv[...], preferred_element_type=jnp.float32)
            for j in range(2):
                vhead[j, ctx] = full[:, j * HEAD_WIDTH : (j + 1) * HEAD_WIDTH].astype(jnp.bfloat16)

    def project_q(half, w, side, ctx):
        full = jnp.dot(xbuf[side, ctx], w[...], preferred_element_type=jnp.float32)
        for h in range(2):
            head = full[:, h * HEAD_WIDTH : (h + 1) * HEAD_WIDTH]
            qbuf[ctx, side, 2 * half + h] = rotate(head, side).astype(jnp.bfloat16)

    def project_side(side, ctx):
        project_q(0, wqa, side, ctx)
        project_q(1, wqb, side, ctx)

    def scores(keys, ctx, side):
        queries = qbuf[ctx, side].reshape(TALL, HEAD_WIDTH)
        return lax.dot_general(
            keys, queries, (((1,), (1,)), ((), ())), preferred_element_type=jnp.float32
        )

    def weigh(values, p):
        return lax.dot_general(
            values, p.astype(jnp.bfloat16), (((0,), (0,)), ((), ())), preferred_element_type=jnp.float32
        )

    def visible(side, first_key, shape, newest):
        key = lax.broadcasted_iota(jnp.int32, shape, 0) + first_key
        token = lax.broadcasted_iota(jnp.int32, shape, 1) % SLAB + side * SLAB
        return key <= token if newest else key > token

    def begin(ctx, side):
        count = (side + 1) * SLAB
        keys = kbuf[0, ctx].reshape(PAIR, HEAD_WIDTH)[:count]
        values = vbuf[0, ctx].reshape(PAIR, HEAD_WIDTH)[:count]
        s = scores(keys, ctx, side)
        s = jnp.where(visible(side, 0, s.shape, True), s, negative_bound)
        m = jnp.max(s, axis=0, keepdims=True)
        p = jnp.exp2((s - m) * SCORE_SCALE)
        top[ctx, side] = m
        total[ctx, side] = jnp.sum(p, axis=0, keepdims=True)
        acc[ctx, side] = weigh(values, p)

    def update(ctx, side, s, values):
        old = top[ctx, side]
        m = jnp.maximum(old, jnp.max(s, axis=0, keepdims=True))
        factor = jnp.exp2((old - m) * SCORE_SCALE)
        p = jnp.exp2((s - m) * SCORE_SCALE)
        top[ctx, side] = m
        total[ctx, side] = total[ctx, side] * factor + jnp.sum(p, axis=0, keepdims=True)
        acc[ctx, side] = acc[ctx, side] * factor + weigh(values, p)

    def middle(ctx, side, level, count=1):
        keys = kbuf[pl.ds(level, count), ctx].reshape(count * PAIR, HEAD_WIDTH)
        values = vbuf[pl.ds(level, count), ctx].reshape(count * PAIR, HEAD_WIDTH)
        update(ctx, side, scores(keys, ctx, side), values)

    def oldest(ctx, side):
        first = side * SLAB
        keys = kbuf[LEVELS, ctx].reshape(PAIR, HEAD_WIDTH)[first:]
        values = vbuf[LEVELS, ctx].reshape(PAIR, HEAD_WIDTH)[first:]
        s = scores(keys, ctx, side)
        s = jnp.where(visible(side, first, s.shape, False), s, negative_bound)
        update(ctx, side, s, values)

    def attend(side, ctx, first, last):
        if first == 0:
            for static in range(2):
                pl.when(side == static)(functools.partial(begin, ctx, static))
        start = max(first, 1)
        if last > start:

            @pl.when(z >= last)
            def _():
                middle(ctx, side, start, last - start + 1)

        if last >= start:

            @pl.when((z < last) | (last == start))
            def _():
                lax.fori_loop(
                    start, jnp.minimum(z, last) + 1,
                    lambda level, c: (middle(ctx, side, level), c)[1], 0,
                )

    def conclude(ctx, side):
        for static in range(2):
            pl.when((z >= LEVELS) & (side == static))(functools.partial(oldest, ctx, static))
        result = (acc[ctx, side] / total[ctx, side]).T
        for h in range(GROUP):
            stage[side, ctx, :, h * HEAD_WIDTH : (h + 1) * HEAD_WIDTH] = result[
                h * SLAB : (h + 1) * SLAB
            ].astype(jnp.bfloat16)

    def out_columns(head):
        return out_ref.at[:, pl.ds(pl.multiple_of(head * 512, 512), 512)]

    head = 2 * core + pick

    def out_far(turn):
        to = (x_near, x_diag)[turn]
        return remote(stage.at[1 - lo, order[turn]], out_columns(head), OUT + turn, to)

    def out_partner():
        return remote(stage.at[lo, 1 - core], out_columns(head), OUT + 2, partner)

    def out_local():
        return pltpu.make_async_copy(stage.at[lo, core], out_columns(head), local.at[5])

    def close_far(turn):
        conclude(order[turn], 1 - lo)
        out_far(turn).start()

    def close_own(turn):
        conclude(order[turn], lo)
        if turn == 0:
            out_local().start()
        else:
            out_partner().start()

    def out_finish():
        out_local().wait()
        out_partner().wait_send()
        landed = out_columns(2 * (1 - core) + pick)
        remote(landed, landed, OUT + 2, partner).wait_recv()
        for turn in range(2):
            out_far(turn).wait_send()
            landed = out_columns(2 * order[turn] + 1 - pick)
            remote(landed, landed, OUT + turn, x_near).wait_recv()

    first, second = order
    far = 1 - lo

    def x_go(*chunks):
        for i in chunks:
            x_near_out(i).start()

    k.p0()
    x_go(0, 1, 2)
    rope_tables()
    k.p1()
    k.p2()
    qb.p0()
    k.p3()
    qb.p1()
    x_local.wait()
    x_in.wait_recv()
    k.p4()
    project_k()
    k0.open(True)
    k1.open(True)
    x_go(3, 4)
    qb.p2()
    v.p0()
    k0.level(0)
    k1.level(0)
    kb0.hop(0)
    kb1.hop(0)
    qb.p3()
    v.p1()
    x_go(5)
    k0.level(1)
    k1.level(1)
    v.p2()
    qa.p0()
    k0.level(2)
    k1.level(2)
    kb0.hop(1)
    kb1.hop(1)
    v.p3()
    project_v()
    v0.open(True)
    v1.open(True)
    x_go(6, 7)
    k0.level(3)
    k1.level(3)
    qa.p1()
    v0.level(0)
    v1.level(0)
    vb0.hop(0)
    vb1.hop(0)
    kb0.hop(2)
    kb1.hop(2)
    qb.p4()
    project_q(1, wqb, lo, first)
    project_q(1, wqb, lo, second)
    qa.p2()
    v0.level(1)
    v1.level(1)
    vb0.hop(1)
    vb1.hop(1)
    k0.level(4)
    k1.level(4)
    kb0.hop(3)
    kb1.hop(3)
    x_pass(0)
    qa.p3()
    project_q(0, wqa, lo, first)
    v0.level(2)
    project_q(0, wqa, lo, second)
    vb0.hop(2)
    attend(lo, first, 0, 1)
    v1.level(2)
    vb1.hop(2)
    attend(lo, second, 0, 0)
    x_pass(1)
    project_side(far, first)
    v0.level(3)
    vb0.hop(3)
    attend(far, first, 0, 2)
    v1.level(3)
    vb1.hop(3)
    attend(far, first, 3, 3)
    kb0.hop(4)
    kb1.hop(4)
    vb0.hop(4)
    v0.level(4)
    close_far(0)
    x_got()
    project_side(far, second)
    attend(far, second, 0, 3)
    vb1.hop(4)
    v1.level(4)
    close_far(1)
    attend(lo, first, 2, 3)
    close_own(0)
    attend(lo, second, 1, 3)
    close_own(1)

    for piece in pieces:
        piece.finish()
    x_out.wait_send()
    for i in range(X_CHUNKS):
        x_near_out(i).wait_send()
    for piece in range(2):
        x_forward(piece, core).wait_send()
    for chain in (*chains, kb0, kb1, vb0, vb1):
        chain.finish()
    out_finish()


def body(hidden_states, query_weight, key_matrix, value_matrix, context_lengths):
    x = hidden_states[0]
    seq = lax.axis_index("seq")
    any_space = pl.BlockSpec(memory_space=pl.ANY)
    bf16, f32 = jnp.bfloat16, jnp.float32
    attended = pl.pallas_call(
        kernel,
        out_shape=jax.ShapeDtypeStruct((SLAB, 2048), bf16),
        in_specs=[any_space] * 4,
        out_specs=any_space,
        scratch_shapes=[
            pltpu.VMEM((2, 2, SLAB, DEPTH), bf16),
            pltpu.VMEM((DEPTH, 256), bf16),
            pltpu.VMEM((DEPTH, 256), bf16),
            pltpu.VMEM((DEPTH, 256), bf16),
            pltpu.VMEM((DEPTH, 256), bf16),
            pltpu.VMEM((2, 2, SLAB, HEAD_WIDTH), bf16),
            pltpu.VMEM((2, 2, SLAB, HEAD_WIDTH), bf16),
            pltpu.VMEM((LEVELS + 1, 2, 2, SLAB, HEAD_WIDTH), bf16),
            pltpu.VMEM((LEVELS + 1, 2, 2, SLAB, HEAD_WIDTH), bf16),
            pltpu.VMEM((LEVELS - 1, 2, SLAB, HEAD_WIDTH), bf16),
            pltpu.VMEM((LEVELS - 1, 2, SLAB, HEAD_WIDTH), bf16),
            pltpu.VMEM((2, 2, GROUP, SLAB, HEAD_WIDTH), bf16),
            pltpu.VMEM((2, 2, SLAB, GROUP * HEAD_WIDTH), bf16),
            pltpu.VMEM((2, 2, HEAD_WIDTH, TALL), f32),
            pltpu.VMEM((2, 2, 1, TALL), f32),
            pltpu.VMEM((2, 2, 1, TALL), f32),
            pltpu.VMEM((2, SLAB, HEAD_WIDTH), f32),
            pltpu.VMEM((2, SLAB, HEAD_WIDTH), f32),
            pltpu.SemaphoreType.DMA((FLOWS,)),
            pltpu.SemaphoreType.DMA((FLOWS,)),
            pltpu.SemaphoreType.DMA((6,)),
        ],
        compiler_params=pltpu.CompilerParams(
            collective_id=0, has_side_effects=True, vmem_limit_bytes=56 * 2**20
        ),
        name="gather_project_attend",
    )(x, query_weight, key_matrix, value_matrix)
    positions = seq * SLAB + jnp.arange(SLAB, dtype=jnp.int32)
    valid = positions < context_lengths[0]
    return jnp.where(valid[:, None], attended, jnp.zeros_like(attended))[None]


def solution(mesh):
    return jax.shard_map(
        body,
        mesh=mesh,
        in_specs=(P("dp", "seq", None), P("dp", None), P("dp", None), P("dp", None), P("dp")),
        out_specs=P("dp", "seq", None),
        check_vma=False,
    )
```
